128 devices in a mesh: grp: 4 (over x), seq: 32 (over z, y, core).
Axes of the slice: x: 4, y: 4, z: 4, core: 2. Of those that a mesh axis runs over, the one named last changes fastest.
Arguments:
- queries: bfloat16 [32768, 2048], P(('grp', 'seq')), may hold values from -150 to 150
- key_states: bfloat16 [32768, 2048], P(('grp', 'seq')), may hold values from -6 to 6
- value_states: bfloat16 [32768, 2048], P(('grp', 'seq')), may hold values from -6 to 6
- attn_out: bfloat16 [32768, 2048], P(('grp', 'seq')), may hold values from -6 to 6
- out_grad: bfloat16 [32768, 2048], P(('grp', 'seq')), may hold values from -6 to 6
- owner_ids: int32 [4, 16], replicated, may hold values from 0 to 31, as said below
Outputs:
- query_grad: bfloat16 [32768, 2048], P(('grp', 'seq'))
- key_grad: bfloat16 [32768, 2048], P(('grp', 'seq'))
- value_grad: bfloat16 [32768, 2048], P(('grp', 'seq'))
The draws below stay inside these ranges and needn't reach their ends.
Inputs may be any that keep to these rules, and one draw needn't show every extreme that they name: In each group the owners never decrease along the blocks (owner_ids[g, b] <= owner_ids[g, b + 1]), so a shard's blocks are consecutive; every shard holds at most 2 blocks, and in every group some shard holds exactly 2.
All inputs are finite; a program needn't handle non-finite values.
Results may differ from the reference program's by a relative error of at most 0.005.
Values may be sent and summed in bfloat16 or wider, within the bound.
A program may use at most 128 MiB of HBM per device.

```python
import jax
import jax.numpy as jnp
from jax import lax

HEADS = 16
HD = 128
BLK = 128
HOPS = 3
FEAT = 2048
CAP = 2
SL = 256
NBLK = 16
ROWS = 32768
N_GRP = 4
N_SEQ = 32


def draw_key_states(key, part):
    key = jax.random.fold_in(key, 3)
    drawn = jnp.clip(jax.random.normal(key, (ROWS, FEAT), jnp.float32), -6.0, 6.0)
    return drawn.astype(jnp.bfloat16)


def draw_queries(key, part):
    key = jax.random.fold_in(key, 5)
    drawn = jnp.clip(jax.random.normal(key, (ROWS, FEAT), jnp.float32), -6.0, 6.0)
    return drawn.astype(jnp.bfloat16)


def owners_of_group(group_key):
    first_key, second_key = jax.random.split(group_key)
    shard_index = jnp.arange(N_SEQ, dtype=jnp.int32)
    busiest = jax.random.randint(first_key, (), 0, N_SEQ)
    counts = jnp.where(shard_index == busiest, CAP, 0).astype(jnp.int32)

    def place_block(step, held):
        priority = jax.random.randint(jax.random.fold_in(second_key, step), (N_SEQ,), 0, 1 << 20) * N_SEQ + shard_index
        priority = jnp.where(held < CAP, priority, -1)
        chosen = jnp.argmax(priority)
        return held + (shard_index == chosen).astype(jnp.int32)
    counts = lax.fori_loop(0, NBLK - CAP, place_block, counts)
    ends = jnp.cumsum(counts)
    block_index = jnp.arange(NBLK, dtype=jnp.int32)
    return jnp.sum((ends[None, :] <= block_index[:, None]).astype(jnp.int32), axis=1)


def draw_owner_ids(key, part):
    key = jax.random.fold_in(key, 7)
    return jax.vmap(owners_of_group)(jax.random.split(key, N_GRP)).astype(jnp.int32)


def shard_levels(key, dims, cuts, low, high):
    loudness = 1.0
    for axis_at, blocks in cuts:
        steps = jax.random.uniform(jax.random.fold_in(jax.random.fold_in(key, 6), axis_at), (blocks,), jnp.float32, low / len(cuts), high / len(cuts))
        loudness = loudness * jnp.repeat(jnp.exp(steps), dims[axis_at] // blocks).reshape((-1,) + (1,) * (len(dims) - 1 - axis_at))
    return loudness


def normal_values(rng, extent, spread, reach, cuts=(), kind=jnp.bfloat16):
    values = jax.random.normal(rng, extent, jnp.float32) * spread
    if len(cuts) > 0:
        values = shard_levels(rng, extent, cuts, -0.22, 0.18) * values
    return jnp.clip(values, min=-reach, max=reach).astype(kind)


def setup_inputs(seed: int = 0) -> dict:
    splits = jax.random.split(jax.random.key(seed), 7)
    queries = draw_queries(jax.random.fold_in(splits[6], 71), 0)
    key_states = draw_key_states(jax.random.fold_in(splits[6], 71), 0)
    value_states = normal_values(splits[2], (ROWS, FEAT), 1.0, 6.0, ((0, 128),))
    attn_out = normal_values(splits[3], (ROWS, FEAT), 1.0, 6.0, ((0, 128),))
    out_grad = normal_values(splits[4], (ROWS, FEAT), 1.0, 6.0, ((0, 128),))
    owner_ids = draw_owner_ids(jax.random.fold_in(splits[6], 71), 0)
    return dict(queries=queries, key_states=key_states, value_states=value_states, attn_out=attn_out, out_grad=out_grad, owner_ids=owner_ids)


def live_rows(counts, row_count):
    block_idx = jnp.arange(row_count, dtype=jnp.int32) // BLK
    return block_idx[None, :] < counts[:, None]


def log_total(scores, allowed):
    masked = jnp.where(allowed, scores, -1e30)
    row_max = jnp.max(masked, axis=-1, keepdims=True)
    return row_max[..., 0] + jnp.log(jnp.sum(jnp.exp(masked - row_max), axis=-1))


def rounded(array):
    return lax.optimization_barrier(array.astype(jnp.bfloat16)).astype(jnp.float32)


def reference(queries, key_states, value_states, attn_out, out_grad, owner_ids):
    shard_total = N_GRP * N_SEQ
    inv_root = HD ** -0.5
    shard_ids = jnp.arange(N_SEQ, dtype=jnp.int32)
    counts = jnp.sum((owner_ids[:, :, None] == shard_ids[None, None, :]).astype(jnp.int32), axis=1).reshape(shard_total)
    live_mask = live_rows(counts, SL)

    def to_heads(array):
        return array.astype(jnp.float32).reshape(shard_total, SL, HEADS, HD)

    q_heads = to_heads(queries)
    k_heads = to_heads(key_states)
    v_heads = to_heads(value_states)
    o_heads = to_heads(attn_out)
    g_heads = to_heads(out_grad)
    empty_rows = jnp.zeros((HOPS, SL, HEADS, HD), jnp.float32)
    empty_live = jnp.zeros((HOPS, SL), bool)
    k_early = jnp.concatenate([empty_rows, k_heads], axis=0)
    v_early = jnp.concatenate([empty_rows, v_heads], axis=0)
    live_early = jnp.concatenate([empty_live, live_mask], axis=0)
    row_index = jnp.arange(SL, dtype=jnp.int32)
    window_index = jnp.arange((HOPS + 1) * SL, dtype=jnp.int32)
    window_back = HOPS - window_index // SL
    window_row = window_index % SL

    def query_side(shard):
        key_win = lax.dynamic_slice_in_dim(k_early, shard, HOPS + 1, 0).reshape((HOPS + 1) * SL, HEADS, HD)
        value_win = lax.dynamic_slice_in_dim(v_early, shard, HOPS + 1, 0).reshape((HOPS + 1) * SL, HEADS, HD)
        live_win = lax.dynamic_slice_in_dim(live_early, shard, HOPS + 1, 0).reshape(-1)
        query_own = lax.dynamic_index_in_dim(q_heads, shard, 0, keepdims=False)
        grad_own = lax.dynamic_index_in_dim(g_heads, shard, 0, keepdims=False)
        out_own = lax.dynamic_index_in_dim(o_heads, shard, 0, keepdims=False)
        live_own = lax.dynamic_index_in_dim(live_mask, shard, 0, keepdims=False)
        allowed = live_own[:, None] & live_win[None, :] & ((window_back[None, :] > 0) | (window_row[None, :] <= row_index[:, None]))
        scores = jnp.einsum('ihd,jhd->hij', query_own, key_win) * inv_root
        log_sum = log_total(scores, allowed[None])
        row_delta = jnp.sum(grad_own * out_own, axis=-1).T
        probs = jnp.where(allowed[None], jnp.exp(scores - log_sum[..., None]), 0.0)
        prob_grad = jnp.einsum('ihd,jhd->hij', grad_own, value_win)
        score_grad = rounded(probs * (prob_grad - row_delta[..., None]))
        query_grad = jnp.einsum('hij,jhd->ihd', score_grad, key_win) * inv_root
        return query_grad.reshape(SL, HEADS * HD).astype(jnp.bfloat16), log_sum, row_delta

    query_grad, log_sums, row_deltas = lax.map(query_side, jnp.arange(shard_total, dtype=jnp.int32))
    q_late = jnp.concatenate([q_heads, empty_rows], axis=0)
    g_late = jnp.concatenate([g_heads, empty_rows], axis=0)
    empty_stats = jnp.zeros((HOPS, HEADS, SL), jnp.float32)
    sum_late = jnp.concatenate([log_sums, empty_stats], axis=0)
    delta_late = jnp.concatenate([row_deltas, empty_stats], axis=0)
    live_late = jnp.concatenate([live_mask, empty_live], axis=0)
    query_ahead = window_index // SL

    def key_side(shard):
        query_win = lax.dynamic_slice_in_dim(q_late, shard, HOPS + 1, 0).reshape((HOPS + 1) * SL, HEADS, HD)
        grad_win = lax.dynamic_slice_in_dim(g_late, shard, HOPS + 1, 0).reshape((HOPS + 1) * SL, HEADS, HD)
        sum_win = lax.dynamic_slice_in_dim(sum_late, shard, HOPS + 1, 0).transpose(1, 0, 2).reshape(HEADS, -1)
        delta_win = lax.dynamic_slice_in_dim(delta_late, shard, HOPS + 1, 0).transpose(1, 0, 2).reshape(HEADS, -1)
        live_win = lax.dynamic_slice_in_dim(live_late, shard, HOPS + 1, 0).reshape(-1)
        key_own = lax.dynamic_index_in_dim(k_heads, shard, 0, keepdims=False)
        value_own = lax.dynamic_index_in_dim(v_heads, shard, 0, keepdims=False)
        live_own = lax.dynamic_index_in_dim(live_mask, shard, 0, keepdims=False)
        allowed = live_win[:, None] & live_own[None, :] & ((query_ahead[:, None] > 0) | (row_index[None, :] <= window_row[:, None]))
        scores = jnp.einsum('ihd,jhd->hij', query_win, key_own) * inv_root
        probs = jnp.where(allowed[None], jnp.exp(scores - sum_win[..., None]), 0.0)
        prob_grad = jnp.einsum('ihd,jhd->hij', grad_win, value_own)
        score_grad = rounded(probs * (prob_grad - delta_win[..., None]))
        prob_bf = rounded(probs)
        key_grad = jnp.einsum('hij,ihd->jhd', score_grad, query_win) * inv_root
        value_grad = jnp.einsum('hij,ihd->jhd', prob_bf, grad_win)
        return key_grad.reshape(SL, HEADS * HD).astype(jnp.bfloat16), value_grad.reshape(SL, HEADS * HD).astype(jnp.bfloat16)

    key_grad, value_grad = lax.map(key_side, jnp.arange(shard_total, dtype=jnp.int32))
    return (query_grad.reshape(ROWS, FEAT), key_grad.reshape(ROWS, FEAT), value_grad.reshape(ROWS, FEAT))
```

```python
import functools
import math

import jax
import jax.numpy as jnp
from jax import lax
from jax.experimental import pallas as pl
from jax.experimental.pallas import tpu as pltpu
from jax.sharding import PartitionSpec as P

HD = 128
BLK = 128
SL = 256
MESH = pl.DeviceIdType.MESH
F32 = jnp.float32
BF16 = jnp.bfloat16
NEG = -1e30
KEY, VAL, QRY, GRD, OUT = range(5)


def dot(a, b, dims):
    return lax.dot_general(a, b, (dims, ((), ())), preferred_element_type=F32)


def kernel(w, nh, owners, q_in, k_in, v_in, o_in, g_in, dq_out, dk_out, dv_out,
           own, kv_out, kv_in, back_out, back_in, part_far, part_own, stage,
           s_buf, dp_buf, p_buf, ds_buf,
           loc_sem, xs_sem, xr_sem, as_sem, ar_sem, bs_sem, br_sem,
           ras_sem, rar_sem, rbs_sem, rbr_sem, ol_sem, os_sem, or_sem):
    n_seq = lax.axis_size("seq")
    n_all = lax.axis_size("grp") * n_seq
    me = lax.axis_index("grp") * n_seq + lax.axis_index("seq")
    core = lax.rem(me, 2)
    even = me - core
    na = w - 2

    def dev(d):
        d = lax.rem(d + n_all, n_all)
        return (d // n_seq, lax.rem(d, n_seq))

    mate = dev(even + 1 - core)
    ahead = dev(me + 2)
    behind = dev(me - 2)

    barrier = pltpu.get_barrier_semaphore()
    for other in (mate, ahead, behind):
        pl.semaphore_signal(barrier, inc=1, device_id=other, device_id_type=MESH)

    inputs = (k_in, v_in, q_in, g_in, o_in)
    outputs = (dq_out, dk_out, dv_out)

    def cols(which_core, h):
        return pl.ds(pl.multiple_of((which_core * nh + h) * HD, HD), HD)

    mine = pl.ds(pl.multiple_of(core * SL, SL), SL)
    mates = pl.ds(pl.multiple_of((1 - core) * SL, SL), SL)

    def local_in(h, a):
        return pltpu.make_async_copy(inputs[a].at[:, cols(core, h)], own.at[h, a, mine], loc_sem.at[h, a])

    def mate_in(h, a):
        return pltpu.make_async_remote_copy(
            src_ref=inputs[a].at[:, cols(1 - core, h)], dst_ref=own.at[h, a, mine],
            send_sem=xs_sem.at[h, a], recv_sem=xr_sem.at[h, a], device_id=mate, device_id_type=MESH)

    def mate_in_arrival(h, a):
        return pltpu.make_async_remote_copy(
            src_ref=own.at[h, a, mates], dst_ref=own.at[h, a, mates],
            send_sem=xs_sem.at[h, a], recv_sem=xr_sem.at[h, a], device_id=mate, device_id_type=MESH)

    def hop(src, dst, h, lo, size, ss, rs, to):
        return pltpu.make_async_remote_copy(
            src_ref=src.at[h, pl.ds(lo, size)], dst_ref=dst.at[h, pl.ds(lo, size)],
            send_sem=ss.at[h], recv_sem=rs.at[h], device_id=to, device_id_type=MESH)

    def send_a(h):
        return hop(kv_out, kv_in, h, 0, na, as_sem, ar_sem, ahead)

    def send_b(h):
        return hop(kv_out, kv_in, h, na, 2, bs_sem, br_sem, ahead)

    def back_a(h):
        return hop(back_out, back_in, h, 0, na, ras_sem, rar_sem, behind)

    def back_b(h):
        return hop(back_out, back_in, h, na, 2, rbs_sem, rbr_sem, behind)

    def local_res(h, a):
        return pltpu.make_async_copy(stage.at[h, a, mine], outputs[a].at[:, cols(core, h)], ol_sem.at[h, a])

    def mate_res(h, a):
        return pltpu.make_async_remote_copy(
            src_ref=stage.at[h, a, mates], dst_ref=outputs[a].at[:, cols(core, h)],
            send_sem=os_sem.at[h, a], recv_sem=or_sem.at[h, a], device_id=mate, device_id_type=MESH)

    def mate_res_arrival(h, a):
        return pltpu.make_async_remote_copy(
            src_ref=stage.at[h, a, mates], dst_ref=outputs[a].at[:, cols(1 - core, h)],
            send_sem=os_sem.at[h, a], recv_sem=or_sem.at[h, a], device_id=mate, device_id_type=MESH)

    def live_count(shard):
        s = jnp.maximum(shard, 0)
        total = jnp.int32(0)
        for b in range(owners.shape[1]):
            total += (owners[s // n_seq, b] == lax.rem(s, n_seq)).astype(jnp.int32)
        return jnp.where(shard >= 0, total, 0)

    c_m3, c_m2, c_m1, c_e, c_o = [live_count(even + i) for i in (-3, -2, -1, 0, 1)]
    own_live = (c_e >= 1, c_e >= 2, c_o >= 1, c_o >= 2)

    def arrived_kind(t):
        passed = jnp.bool_(False)
        if t == w - 1:
            passed = c_m3 >= 1
        elif t == w - 2:
            passed = c_m3 >= 2
        own_there = c_m1 + c_m2 > t
        return passed, own_there

    near_ok = []
    far_ok = []
    for t in range(w):
        passed, own_there = arrived_kind(t)
        near_ok.append(jnp.logical_or(passed, own_there))
        far_ok.append(jnp.logical_and(jnp.logical_not(passed), own_there))

    def fetch(h, a_list):
        for a in a_list:
            local_in(h, a).start()
            mate_in(h, a).start()

    def fetched(h, a_list):
        for a in a_list:
            local_in(h, a).wait()
            mate_in_arrival(h, a).wait_recv()

    def own_block(h, a, slot):
        return own[h, a, slot * BLK:(slot + 1) * BLK, :]

    def own_pick(h, x, t):
        e0, e1, o0, o1 = 0, 1, 2, 3
        if t == 0:
            return jnp.where(c_o >= 1, own_block(h, x, o0), own_block(h, x, e0))
        if t == 1:
            return jnp.where(c_o >= 2, own_block(h, x, o1),
                             jnp.where(c_o >= 1, own_block(h, x, e0), own_block(h, x, e1)))
        if t == 2:
            return jnp.where(c_o >= 2, own_block(h, x, e0), own_block(h, x, e1))
        return own_block(h, x, e1)

    def make_a(h):
        for t in range(na):
            for x in (KEY, VAL):
                kv_out[h, t, x] = own_pick(h, x, t)

    def make_b(h):
        for x in (KEY, VAL):
            first, second = kv_in[h, 0, x], kv_in[h, 1, x]
            if w - 2 < 4:
                second = jnp.where(c_m1 >= 2, second, own_pick(h, x, w - 2))
            if w - 1 < 4:
                first = jnp.where(c_m1 >= 1, first, own_pick(h, x, w - 1))
            kv_out[h, w - 2, x] = second
            kv_out[h, w - 1, x] = first

    inv_root = HD ** (-0.5)
    exp_scale = inv_root * math.log2(math.e)
    row_id = lax.broadcasted_iota(jnp.int32, (BLK, SL), 0)
    col_id = lax.broadcasted_iota(jnp.int32, (BLK, SL), 1)
    first_half = lax.broadcasted_iota(jnp.int32, (1, SL), 1) < BLK

    def compute(h):
        keys, vals = own[h, KEY], own[h, VAL]
        far_keys = kv_in[h, :, KEY].reshape(w * BLK, HD)
        far_vals = kv_in[h, :, VAL].reshape(w * BLK, HD)
        prod = own[h, GRD].astype(F32) * own[h, OUT].astype(F32)
        delta_all = jnp.sum(prod.T, axis=0, keepdims=True)
        for a in range(2):
            nk = SL * (a + 1)
            rows = slice(a * SL, (a + 1) * SL)
            query, grad = own[h, QRY, rows], own[h, GRD, rows]
            delta = delta_all[:, rows]
            s_buf[0:nk] = dot(keys[:nk], query, ((1,), (1,)))
            s_buf[2 * SL:] = dot(far_keys, query, ((1,), (1,)))
            dp_buf[0:nk] = dot(vals[:nk], grad, ((1,), (1,)))
            dp_buf[2 * SL:] = dot(far_vals, grad, ((1,), (1,)))
            blocks = list(range(nk // BLK)) + [4 + t for t in range(w)]
            top = None
            for b in blocks:
                at = slice(b * BLK, (b + 1) * BLK)
                if b >= 4:
                    ok = (near_ok, far_ok)[a][b - 4]
                else:
                    ok = own_live[b]
                x = s_buf[at] + jnp.where(ok, 0.0, NEG).astype(F32)
                if b < 4 and b >= 2 * a:
                    x = jnp.where(row_id + (b - 2 * a) * BLK <= col_id, x, NEG)
                s_buf[at] = x
                high = jnp.max(x, axis=0, keepdims=True)
                top = high if top is None else jnp.maximum(top, high)
            total = None
            for b in blocks:
                at = slice(b * BLK, (b + 1) * BLK)
                e = jnp.exp2((s_buf[at] - top) * exp_scale)
                s_buf[at] = e
                part = jnp.sum(e, axis=0, keepdims=True)
                total = part if total is None else total + part
            live = jnp.where(first_half, jnp.where(own_live[2 * a], 1.0, 0.0).astype(F32),
                             jnp.where(own_live[2 * a + 1], 1.0, 0.0).astype(F32))
            scale = live / total
            for b in blocks:
                at = slice(b * BLK, (b + 1) * BLK)
                prob = s_buf[at] * scale
                p_buf[at, rows] = prob.astype(BF16)
                ds_buf[at, rows] = (prob * (dp_buf[at] - delta)).astype(BF16)
            dq = dot(ds_buf[0:nk, rows], keys[:nk], ((0,), (0,)))
            dq += dot(ds_buf[2 * SL:, rows], far_keys, ((0,), (0,)))
            stage[h, 0, rows] = (dq * inv_root).astype(BF16)
        second = slice(SL, 2 * SL)
        query, grad = own[h, QRY], own[h, GRD]
        nat = ((1,), (0,))
        part_own[h, 0, 0:SL] = dot(ds_buf[0:SL], query, nat) * inv_root
        part_own[h, 0, second] = dot(ds_buf[second, second], query[second], nat) * inv_root
        part_own[h, 1, 0:SL] = dot(p_buf[0:SL], grad, nat)
        part_own[h, 1, second] = dot(p_buf[second, second], grad[second], nat)
        far = slice(2 * SL, (4 + na) * BLK)
        part_far[h, :, 0] = (dot(ds_buf[far], query, nat) * inv_root).reshape(na, BLK, HD)
        part_far[h, :, 1] = dot(p_buf[far], grad, nat).reshape(na, BLK, HD)
        far = slice((4 + na) * BLK, (4 + w) * BLK)
        back_out[h, na:w, 0] = (dot(ds_buf[far], query, nat) * inv_root).astype(BF16).reshape(2, BLK, HD)
        back_out[h, na:w, 1] = dot(p_buf[far], grad, nat).astype(BF16).reshape(2, BLK, HD)

    def back_sums(h):
        for x in range(2):
            for t in range(na):
                term = part_far[h, t, x]
                if t == 0:
                    term += jnp.where(c_m1 >= 1, back_in[h, w - 1, x].astype(F32), 0.0)
                if t == 1:
                    term += jnp.where(c_m1 >= 2, back_in[h, w - 2, x].astype(F32), 0.0)
                back_out[h, t, x] = term.astype(BF16)

    def finish(h):
        for x in range(2):
            got = [back_in[h, t, x].astype(F32) for t in range(4)]
            adds = (
                jnp.where(c_e >= 1, jnp.where(c_o >= 2, got[2], jnp.where(c_o >= 1, got[1], got[0])), 0.0),
                jnp.where(c_e >= 2, jnp.where(c_o >= 2, got[3], jnp.where(c_o >= 1, got[2], got[1])), 0.0),
                jnp.where(c_o >= 1, got[0], 0.0),
                jnp.where(c_o >= 2, got[1], 0.0),
            )
            for b in range(4):
                at = slice(b * BLK, (b + 1) * BLK)
                stage[h, 1 + x, at] = (part_own[h, x, at] + adds[b]).astype(BF16)

    pl.semaphore_wait(barrier, 3)
    early = min(2, nh)
    for h in range(early):
        fetch(h, (KEY, VAL))
    for h in range(early):
        fetched(h, (KEY, VAL))
        make_a(h)
        send_a(h).start()
    for h in range(early):
        fetch(h, (QRY, GRD, OUT))

    @pl.loop(early, nh)
    def _(h):
        fetch(h, (KEY, VAL, QRY, GRD, OUT))

    @pl.loop(0, nh + 3)
    def _(step):
        @pl.when(step < nh)
        def _():
            h = step
            send_a(h).wait_recv()
            make_b(h)
            send_b(h).start()

        @pl.when(step + early < nh)
        def _():
            h = step + early
            fetched(h, (KEY, VAL))
            make_a(h)
            send_a(h).start()

        @pl.when(jnp.logical_and(step >= 1, step <= nh))
        def _():
            h = step - 1
            fetched(h, (QRY, GRD, OUT))
            send_b(h).wait_recv()
            compute(h)
            back_b(h).start()
            local_res(h, 0).start()
            mate_res(h, 0).start()

        @pl.when(jnp.logical_and(step >= 2, step <= nh + 1))
        def _():
            h = step - 2
            back_b(h).wait_recv()
            back_sums(h)
            back_a(h).start()

        @pl.when(step >= 3)
        def _():
            h = step - 3
            back_a(h).wait_recv()
            finish(h)
            for a in (1, 2):
                local_res(h, a).start()
                mate_res(h, a).start()

    @pl.loop(0, nh)
    def _(h):
        for a in range(5):
            mate_in(h, a).wait_send()
        send_a(h).wait_send()
        send_b(h).wait_send()
        back_a(h).wait_send()
        back_b(h).wait_send()
        for a in range(3):
            local_res(h, a).wait()
            mate_res(h, a).wait_send()
            mate_res_arrival(h, a).wait_recv()


def fused(w, owners, queries, key_states, value_states, attn_out, out_grad):
    width = queries.shape[1]
    nh = width // (2 * HD)
    anywhere = pl.BlockSpec(memory_space=pl.ANY)
    dma = pltpu.SemaphoreType.DMA
    slots = pltpu.VMEM((nh, w, 2, BLK, HD), BF16)
    return pl.pallas_call(
        functools.partial(kernel, w, nh),
        out_shape=[jax.ShapeDtypeStruct(queries.shape, BF16)] * 3,
        in_specs=[pl.BlockSpec(memory_space=pltpu.SMEM)] + [anywhere] * 5,
        out_specs=[anywhere] * 3,
        scratch_shapes=[
            pltpu.VMEM((nh, 5, 2 * SL, HD), BF16),
            slots, slots, slots, slots,
            pltpu.VMEM((nh, w - 2, 2, BLK, HD), F32),
            pltpu.VMEM((nh, 2, 2 * SL, HD), F32),
            pltpu.VMEM((nh, 3, 2 * SL, HD), BF16),
            pltpu.VMEM(((4 + w) * BLK, SL), F32),
            pltpu.VMEM(((4 + w) * BLK, SL), F32),
            pltpu.VMEM(((4 + w) * BLK, 2 * SL), BF16),
            pltpu.VMEM(((4 + w) * BLK, 2 * SL), BF16),
            dma((nh, 5)), dma((nh, 5)), dma((nh, 5)),
            dma((nh,)), dma((nh,)), dma((nh,)), dma((nh,)),
            dma((nh,)), dma((nh,)), dma((nh,)), dma((nh,)),
            dma((nh, 3)), dma((nh, 3)), dma((nh, 3)),
        ],
        compiler_params=pltpu.CompilerParams(
            collective_id=w - 4, has_side_effects=True, vmem_limit_bytes=56 * 2**20),
        name="slots%d" % w,
    )(owners, queries, key_states, value_states, attn_out, out_grad)


def per_device(queries, key_states, value_states, attn_out, out_grad, owner_ids):
    n_grp, n_seq = lax.axis_size("grp"), lax.axis_size("seq")
    shard = (owner_ids + n_seq * jnp.arange(n_grp, dtype=jnp.int32)[:, None]).reshape(1, -1)
    first = 2 * jnp.arange(n_grp * n_seq // 2 - 1, dtype=jnp.int32)[:, None] - 1
    inside = jnp.logical_and(shard >= first, shard <= first + 2)
    widest = jnp.max(jnp.sum(inside.astype(jnp.int32), axis=1))
    return lax.switch(
        jnp.clip(widest - 4, 0, 2),
        [functools.partial(fused, w) for w in (4, 5, 6)],
        owner_ids, queries, key_states, value_states, attn_out, out_grad)


def solution(mesh):
    rows = P(("grp", "seq"), None)
    return jax.shard_map(
        per_device,
        mesh=mesh,
        in_specs=(rows,) * 5 + (P(),),
        out_specs=(rows,) * 3,
        check_vma=False,
    )
```

```python
import functools
import math

import jax
import jax.numpy as jnp
from jax import lax
from jax.experimental import pallas as pl
from jax.experimental.pallas import tpu as pltpu
from jax.sharding import PartitionSpec as P

HD = 128
BLK = 128
SL = 256
MESH = pl.DeviceIdType.MESH
F32 = jnp.float32
BF16 = jnp.bfloat16
NEG = -1e30
LEAD, QUERY_LAG, KEY_LAG = 2, 1, 2
KEY, VAL, QRY, GRD, OUT = range(5)


def dot(a, b, dims):
    return lax.dot_general(a, b, (dims, ((), ())), preferred_element_type=F32)


def kernel(w, nh, owners, q_in, k_in, v_in, o_in, g_in, dq_out, dk_out, dv_out,
           own, kv_out, kv_in, qg_out, qg_in, stat_out, stat_near, stat_far, part_own, stage,
           s_buf, dp_buf, p_buf, ds_buf, sk_buf, dpk_buf, pk_buf, dsk_buf,
           loc_sem, xs_sem, xr_sem, kas_sem, kar_sem, kbs_sem, kbr_sem, qas_sem, qar_sem, qbs_sem, qbr_sem,
           sns_sem, snr_sem, sfs_sem, sfr_sem, ol_sem, os_sem, or_sem):
    n_seq = lax.axis_size("seq")
    n_all = lax.axis_size("grp") * n_seq
    me = lax.axis_index("grp") * n_seq + lax.axis_index("seq")
    core = lax.rem(me, 2)
    even = me - core
    na = w - 2

    def dev(d):
        d = lax.rem(d + n_all, n_all)
        return (d // n_seq, lax.rem(d, n_seq))

    def only(cond):
        return lambda act: pl.when(cond)(act)

    mate = dev(even + 1 - core)
    ahead, ahead_two, behind, behind_two = [dev(me + i) for i in (2, 4, -2, -4)]
    has_ahead, has_ahead_two = me < n_all - 2, me < n_all - 4
    has_behind, has_behind_two = me >= 2, me >= 4
    when_ahead, when_ahead_two = only(has_ahead), only(has_ahead_two)
    when_behind, when_behind_two = only(has_behind), only(has_behind_two)

    barrier = pltpu.get_barrier_semaphore()
    pl.semaphore_signal(barrier, inc=1, device_id=mate, device_id_type=MESH)
    met = jnp.int32(1)
    for there, other in ((has_ahead, ahead), (has_behind, behind), (has_ahead_two, ahead_two), (has_behind_two, behind_two)):
        @pl.when(there)
        def _():
            pl.semaphore_signal(barrier, inc=1, device_id=other, device_id_type=MESH)

        met += there.astype(jnp.int32)

    inputs = (k_in, v_in, q_in, g_in, o_in)
    outputs = (dq_out, dk_out, dv_out)

    def cols(which_core, h):
        return pl.ds(pl.multiple_of((which_core * nh + h) * HD, HD), HD)

    mine = pl.ds(pl.multiple_of(core * SL, SL), SL)
    mates = pl.ds(pl.multiple_of((1 - core) * SL, SL), SL)

    def local_in(h, a):
        return pltpu.make_async_copy(inputs[a].at[:, cols(core, h)], own.at[h, a, mine], loc_sem.at[h, a])

    def mate_in(h, a):
        return pltpu.make_async_remote_copy(
            src_ref=inputs[a].at[:, cols(1 - core, h)], dst_ref=own.at[h, a, mine],
            send_sem=xs_sem.at[h, a], recv_sem=xr_sem.at[h, a], device_id=mate, device_id_type=MESH)

    def mate_in_arrival(h, a):
        return pltpu.make_async_remote_copy(
            src_ref=own.at[h, a, mates], dst_ref=own.at[h, a, mates],
            send_sem=xs_sem.at[h, a], recv_sem=xr_sem.at[h, a], device_id=mate, device_id_type=MESH)

    def hop(src, dst, h, lo, size, ss, rs, to):
        return pltpu.make_async_remote_copy(
            src_ref=src.at[h, pl.ds(lo, size)], dst_ref=dst.at[h, pl.ds(lo, size)],
            send_sem=ss.at[h], recv_sem=rs.at[h], device_id=to, device_id_type=MESH)

    def keys_a(h):
        return hop(kv_out, kv_in, h, 0, na, kas_sem, kar_sem, ahead)

    def keys_b(h):
        return hop(kv_out, kv_in, h, na, 2, kbs_sem, kbr_sem, ahead)

    def rows_a(h):
        return hop(qg_out, qg_in, h, 0, na, qas_sem, qar_sem, behind)

    def rows_b(h):
        return hop(qg_out, qg_in, h, na, 2, qbs_sem, qbr_sem, behind)

    def stats_near(h):
        return hop(stat_out, stat_near, h, 0, 16, sns_sem, snr_sem, behind)

    def stats_far(h):
        return hop(stat_out, stat_far, h, 0, 16, sfs_sem, sfr_sem, behind_two)

    def local_res(h, a):
        return pltpu.make_async_copy(stage.at[h, a, mine], outputs[a].at[:, cols(core, h)], ol_sem.at[h, a])

    def mate_res(h, a):
        return pltpu.make_async_remote_copy(
            src_ref=stage.at[h, a, mates], dst_ref=outputs[a].at[:, cols(core, h)],
            send_sem=os_sem.at[h, a], recv_sem=or_sem.at[h, a], device_id=mate, device_id_type=MESH)

    def mate_res_arrival(h, a):
        return pltpu.make_async_remote_copy(
            src_ref=stage.at[h, a, mates], dst_ref=outputs[a].at[:, cols(1 - core, h)],
            send_sem=os_sem.at[h, a], recv_sem=or_sem.at[h, a], device_id=mate, device_id_type=MESH)

    def live_count(shard):
        s = jnp.clip(shard, 0, n_all - 1)
        total = jnp.int32(0)
        for b in range(owners.shape[1]):
            total += (owners[s // n_seq, b] == lax.rem(s, n_seq)).astype(jnp.int32)
        return jnp.where(jnp.logical_and(shard >= 0, shard < n_all), total, 0)

    c_m3, c_m2, c_m1, c_e, c_o, c_p2, c_p3, c_p4 = [live_count(even + i) for i in range(-3, 5)]
    own_live = (c_e >= 1, c_e >= 2, c_o >= 1, c_o >= 2)

    def arrivals(passed_count, own_count):
        passed, there = [], []
        for t in range(w):
            by_pass = jnp.bool_(False)
            if t == w - 1:
                by_pass = passed_count >= 1
            elif t == w - 2:
                by_pass = passed_count >= 2
            passed.append(by_pass)
            there.append(jnp.logical_and(jnp.logical_not(by_pass), own_count > t))
        return passed, there

    key_passed, key_own = arrivals(c_m3, c_m1 + c_m2)
    row_passed, row_own = arrivals(c_p4, c_p2 + c_p3)

    def fetch(h, a_list):
        for a in a_list:
            local_in(h, a).start()
            mate_in(h, a).start()

    def fetched(h, a_list):
        for a in a_list:
            local_in(h, a).wait()
            mate_in_arrival(h, a).wait_recv()

    def numbered(t, first_count, first, then):
        if t == 0:
            return jnp.where(first_count >= 1, first(0), then(0))
        if t == 1:
            return jnp.where(first_count >= 2, first(1), jnp.where(first_count >= 1, then(0), then(1)))
        if t == 2:
            return jnp.where(first_count >= 2, then(0), then(1))
        return then(1)

    def own_pick(h, x, t):
        def from_even(i):
            return own[h, x, i * BLK:(i + 1) * BLK, :]

        def from_odd(i):
            return own[h, x, (2 + i) * BLK:(3 + i) * BLK, :]

        if x in (KEY, VAL):
            return numbered(t, c_o, from_odd, from_even)
        return numbered(t, c_e, from_even, from_odd)

    def make_a(h, pair, out):
        for t in range(na):
            for i, x in enumerate(pair):
                out[h, t, i] = own_pick(h, x, t)

    def make_b(h, pair, arrived, out, passed_count):
        for i, x in enumerate(pair):
            first, second = arrived[h, 0, i], arrived[h, 1, i]
            if w - 2 < 4:
                second = jnp.where(passed_count >= 2, second, own_pick(h, x, w - 2))
            if w - 1 < 4:
                first = jnp.where(passed_count >= 1, first, own_pick(h, x, w - 1))
            out[h, w - 2, i] = second
            out[h, w - 1, i] = first

    inv_root = HD ** (-0.5)
    exp_scale = inv_root * math.log2(math.e)
    row_id = lax.broadcasted_iota(jnp.int32, (BLK, SL), 0)
    col_id = lax.broadcasted_iota(jnp.int32, (BLK, SL), 1)
    first_half = lax.broadcasted_iota(jnp.int32, (1, SL), 1) < BLK
    nat, both_last = ((1,), (0,)), ((1,), (1,))

    def block(b):
        return slice(b * BLK, (b + 1) * BLK)

    def query_side(h):
        keys, vals = own[h, KEY], own[h, VAL]
        far_keys = kv_in[h, :, 0].reshape(w * BLK, HD)
        far_vals = kv_in[h, :, 1].reshape(w * BLK, HD)
        prod = own[h, GRD].astype(F32) * own[h, OUT].astype(F32)
        delta_all = jnp.sum(prod.T, axis=0, keepdims=True)
        for a in range(2):
            nk = SL * (a + 1)
            rows = slice(a * SL, (a + 1) * SL)
            query, grad = own[h, QRY, rows], own[h, GRD, rows]
            delta = delta_all[:, rows]
            s_buf[0:nk] = dot(keys[:nk], query, both_last)
            s_buf[2 * SL:] = dot(far_keys, query, both_last)
            dp_buf[0:nk] = dot(vals[:nk], grad, both_last)
            dp_buf[2 * SL:] = dot(far_vals, grad, both_last)
            blocks = list(range(nk // BLK)) + [4 + t for t in range(w)]
            top = None
            for b in blocks:
                if b >= 4:
                    ok = key_own[b - 4]
                    if a == 0:
                        ok = jnp.logical_or(ok, key_passed[b - 4])
                else:
                    ok = own_live[b]
                x = s_buf[block(b)] + jnp.where(ok, 0.0, NEG).astype(F32)
                if b < 4 and b >= 2 * a:
                    x = jnp.where(row_id + (b - 2 * a) * BLK <= col_id, x, NEG)
                s_buf[block(b)] = x
                high = jnp.max(x, axis=0, keepdims=True)
                top = high if top is None else jnp.maximum(top, high)
            total = None
            for b in blocks:
                e = jnp.exp2((s_buf[block(b)] - top) * exp_scale)
                s_buf[block(b)] = e
                part = jnp.sum(e, axis=0, keepdims=True)
                total = part if total is None else total + part
            live = jnp.where(first_half, jnp.where(own_live[2 * a], 1.0, 0.0).astype(F32),
                             jnp.where(own_live[2 * a + 1], 1.0, 0.0).astype(F32))
            scale = live / total
            for i in range(2):
                for r, stat in enumerate((top, scale, delta)):
                    stat_out[h, 4 * r + 2 * a + i:4 * r + 2 * a + i + 1, :] = stat[:, block(i)]
            for b in blocks:
                prob = s_buf[block(b)] * scale
                if b < 4:
                    p_buf[block(b), rows] = prob.astype(BF16)
                ds_buf[block(b), rows] = (prob * (dp_buf[block(b)] - delta)).astype(BF16)
            dq = dot(ds_buf[0:nk, rows], keys[:nk], ((0,), (0,)))
            dq += dot(ds_buf[2 * SL:, rows], far_keys, ((0,), (0,)))
            stage[h, 0, rows] = (dq * inv_root).astype(BF16)

    def own_keys(h):
        second = slice(SL, 2 * SL)
        query, grad = own[h, QRY], own[h, GRD]
        part_own[h, 0, 0:SL] = dot(ds_buf[0:SL], query, nat)
        part_own[h, 0, second] = dot(ds_buf[second, second], query[second], nat)
        part_own[h, 1, 0:SL] = dot(p_buf[0:SL], grad, nat)
        part_own[h, 1, second] = dot(p_buf[second, second], grad[second], nat)

    def key_side(h):
        queries = qg_in[h, :, 0].reshape(w * BLK, HD)
        grads = qg_in[h, :, 1].reshape(w * BLK, HD)
        sk_buf[...] = dot(own[h, KEY], queries, both_last)
        dpk_buf[...] = dot(own[h, VAL], grads, both_last)
        for t in range(w):
            def stat(r):
                def near(i):
                    return stat_near[h, 4 * r + i:4 * r + i + 1, :]

                row = numbered(t, c_p2, near, lambda i: near(2 + i))
                if t == w - 1:
                    row = jnp.where(row_passed[t], stat_far[h, 4 * r:4 * r + 1, :], row)
                if t == w - 2:
                    row = jnp.where(row_passed[t], stat_far[h, 4 * r + 1:4 * r + 2, :], row)
                return row

            top, scale, delta = stat(0), stat(1), stat(2)
            for b in range(4):
                ok = row_own[t]
                if b >= 2:
                    ok = jnp.logical_or(ok, row_passed[t])
                level = jnp.where(jnp.logical_and(ok, own_live[b]), top, -NEG)
                prob = jnp.exp2((sk_buf[block(b), block(t)] - level) * exp_scale) * scale
                pk_buf[block(b), block(t)] = prob.astype(BF16)
                dsk_buf[block(b), block(t)] = (prob * (dpk_buf[block(b), block(t)] - delta)).astype(BF16)
        dk = part_own[h, 0] + dot(dsk_buf[...], queries, nat)
        stage[h, 1] = (dk * inv_root).astype(BF16)
        stage[h, 2] = (part_own[h, 1] + dot(pk_buf[...], grads, nat)).astype(BF16)

    early = min(LEAD, nh)
    for h in range(early):
        for a in (KEY, VAL, QRY, GRD):
            local_in(h, a).start()

    @pl.when(jnp.logical_not(has_behind))
    def _():
        kv_in[...] = jnp.zeros_like(kv_in)

    @pl.when(jnp.logical_not(has_ahead))
    def _():
        qg_in[...] = jnp.zeros_like(qg_in)
        stat_near[...] = jnp.zeros_like(stat_near)

    @pl.when(jnp.logical_not(has_ahead_two))
    def _():
        stat_far[...] = jnp.zeros_like(stat_far)

    pl.semaphore_wait(barrier, met)
    for h in range(early):
        for a in (KEY, VAL, QRY, GRD):
            mate_in(h, a).start()

    def start_a(h):
        fetched(h, (KEY, VAL))

        @when_ahead
        def _():
            make_a(h, (KEY, VAL), kv_out)
            keys_a(h).start()

        fetched(h, (QRY, GRD))

        @when_behind
        def _():
            make_a(h, (QRY, GRD), qg_out)
            rows_a(h).start()

    for h in range(early):
        start_a(h)

    for h in range(early):
        fetch(h, (OUT,))

    @pl.loop(early, nh)
    def _(h):
        fetch(h, (KEY, VAL, QRY, GRD, OUT))

    @pl.loop(0, nh + KEY_LAG)
    def _(step):
        @pl.when(step < nh)
        def _():
            h = step

            @when_behind
            def _():
                keys_a(h).wait_recv()

            @when_ahead
            def _():
                make_b(h, (KEY, VAL), kv_in, kv_out, c_m1)
                keys_b(h).start()
                rows_a(h).wait_recv()

            @when_behind
            def _():
                make_b(h, (QRY, GRD), qg_in, qg_out, c_p2)
                rows_b(h).start()

        @pl.when(step + early < nh)
        def _():
            start_a(step + early)

        @pl.when(jnp.logical_and(step >= QUERY_LAG, step < nh + QUERY_LAG))
        def _():
            h = step - QUERY_LAG
            fetched(h, (OUT,))

            @when_behind
            def _():
                keys_b(h).wait_recv()

            query_side(h)

            @when_behind
            def _():
                stats_near(h).start()

            @when_behind_two
            def _():
                stats_far(h).start()

            local_res(h, 0).start()
            mate_res(h, 0).start()
            own_keys(h)

        @pl.when(step >= KEY_LAG)
        def _():
            h = step - KEY_LAG

            @when_ahead
            def _():
                rows_b(h).wait_recv()
                stats_near(h).wait_recv()

            @when_ahead_two
            def _():
                stats_far(h).wait_recv()

            key_side(h)
            for a in (1, 2):
                local_res(h, a).start()
                mate_res(h, a).start()

    @pl.loop(0, nh)
    def _(h):
        for a in range(5):
            mate_in(h, a).wait_send()

        @when_ahead
        def _():
            keys_a(h).wait_send()
            keys_b(h).wait_send()

        @when_behind
        def _():
            rows_a(h).wait_send()
            rows_b(h).wait_send()
            stats_near(h).wait_send()

        @when_behind_two
        def _():
            stats_far(h).wait_send()

        for a in range(3):
            local_res(h, a).wait()
            mate_res(h, a).wait_send()
            mate_res_arrival(h, a).wait_recv()


def fused(w, owners, queries, key_states, value_states, attn_out, out_grad):
    width = queries.shape[1]
    nh = width // (2 * HD)
    anywhere = pl.BlockSpec(memory_space=pl.ANY)
    dma = pltpu.SemaphoreType.DMA
    slots = pltpu.VMEM((nh, w, 2, BLK, HD), BF16)
    stats = pltpu.VMEM((nh, 16, HD), F32)
    return pl.pallas_call(
        functools.partial(kernel, w, nh),
        out_shape=[jax.ShapeDtypeStruct(queries.shape, BF16)] * 3,
        in_specs=[pl.BlockSpec(memory_space=pltpu.SMEM)] + [anywhere] * 5,
        out_specs=[anywhere] * 3,
        scratch_shapes=[
            pltpu.VMEM((nh, 5, 2 * SL, HD), BF16),
            slots, slots, slots, slots,
            stats, stats, stats,
            pltpu.VMEM((nh, 2, 2 * SL, HD), F32),
            pltpu.VMEM((nh, 3, 2 * SL, HD), BF16),
            pltpu.VMEM(((4 + w) * BLK, SL), F32),
            pltpu.VMEM(((4 + w) * BLK, SL), F32),
            pltpu.VMEM((2 * SL, 2 * SL), BF16),
            pltpu.VMEM(((4 + w) * BLK, 2 * SL), BF16),
            pltpu.VMEM((2 * SL, w * BLK), F32),
            pltpu.VMEM((2 * SL, w * BLK), F32),
            pltpu.VMEM((2 * SL, w * BLK), BF16),
            pltpu.VMEM((2 * SL, w * BLK), BF16),
            dma((nh, 5)), dma((nh, 5)), dma((nh, 5)),
        ] + [dma((nh,))] * 12 + [dma((nh, 3))] * 3,
        compiler_params=pltpu.CompilerParams(
            collective_id=w - 4, has_side_effects=True, vmem_limit_bytes=56 * 2**20),
        name="slots%d" % w,
    )(owners, queries, key_states, value_states, attn_out, out_grad)


def per_device(queries, key_states, value_states, attn_out, out_grad, owner_ids):
    n_grp, n_seq = lax.axis_size("grp"), lax.axis_size("seq")
    shard = (owner_ids + n_seq * jnp.arange(n_grp, dtype=jnp.int32)[:, None]).reshape(-1)
    last = shard + 2 - jnp.logical_or(shard == 0, shard == n_grp * n_seq - 3).astype(jnp.int32)
    five = (shard[4:] <= last[:-4]).astype(jnp.int32)
    six = (jnp.pad(shard[5:], (0, 1), constant_values=n_grp * n_seq + 2) <= last[:-4]).astype(jnp.int32)
    return lax.switch(
        jnp.max(five + six),
        [functools.partial(fused, w) for w in (4, 5, 6)],
        owner_ids, queries, key_states, value_states, attn_out, out_grad)


def solution(mesh):
    rows = P(("grp", "seq"), None)
    return jax.shard_map(
        per_device,
        mesh=mesh,
        in_specs=(rows,) * 5 + (P(),),
        out_specs=(rows,) * 3,
        check_vma=False,
    )
```

```python
import functools
import math

import jax
import jax.numpy as jnp
from jax import lax
from jax.experimental import pallas as pl
from jax.experimental.pallas import tpu as pltpu
from jax.sharding import PartitionSpec as P

HD = 128
BLK = 128
SL = 256
MESH = pl.DeviceIdType.MESH
F32 = jnp.float32
BF16 = jnp.bfloat16
NEG = -1e30
LEAD, QUERY_LAG, KEY_LAG = 2, 1, 3
KEY, VAL, QRY, GRD, OUT = range(5)


def dot(a, b, dims):
    return lax.dot_general(a, b, (dims, ((), ())), preferred_element_type=F32)


def kernel(w, nh, owners, q_in, k_in, v_in, o_in, g_in, dq_out, dk_out, dv_out,
           own, kv_out, kv_in, qg_out, qg_in, stat_out, stat_near, stat_far, part_own, stage,
           s_buf, dp_buf, p_buf, ds_buf, sk_buf, dpk_buf, pk_buf, dsk_buf,
           loc_sem, xs_sem, xr_sem, kas_sem, kar_sem, kbs_sem, kbr_sem, qas_sem, qar_sem, qbs_sem, qbr_sem,
           sns_sem, snr_sem, sfs_sem, sfr_sem, ol_sem, os_sem, or_sem):
    n_seq = lax.axis_size("seq")
    n_all = lax.axis_size("grp") * n_seq
    me = lax.axis_index("grp") * n_seq + lax.axis_index("seq")
    core = lax.rem(me, 2)
    even = me - core
    na = w - 2

    def dev(d):
        d = lax.rem(d + n_all, n_all)
        return (d // n_seq, lax.rem(d, n_seq))

    def only(cond):
        return lambda act: pl.when(cond)(act)

    mate = dev(even + 1 - core)
    ahead, ahead_two, behind, behind_two = [dev(me + i) for i in (2, 4, -2, -4)]
    has_ahead, has_ahead_two = me < n_all - 2, me < n_all - 4
    has_behind, has_behind_two = me >= 2, me >= 4
    when_ahead, when_ahead_two = only(has_ahead), only(has_ahead_two)
    when_behind, when_behind_two = only(has_behind), only(has_behind_two)

    barrier = pltpu.get_barrier_semaphore()
    pl.semaphore_signal(barrier, inc=1, device_id=mate, device_id_type=MESH)
    met = jnp.int32(1)
    for there, other in ((has_ahead, ahead), (has_behind, behind), (has_ahead_two, ahead_two), (has_behind_two, behind_two)):
        @pl.when(there)
        def _():
            pl.semaphore_signal(barrier, inc=1, device_id=other, device_id_type=MESH)

        met += there.astype(jnp.int32)

    inputs = (k_in, v_in, q_in, g_in, o_in)
    outputs = (dq_out, dk_out, dv_out)

    def cols(which_core, h):
        return pl.ds(pl.multiple_of((which_core * nh + h) * HD, HD), HD)

    mine = pl.ds(pl.multiple_of(core * SL, SL), SL)
    mates = pl.ds(pl.multiple_of((1 - core) * SL, SL), SL)

    def local_in(h, a):
        return pltpu.make_async_copy(inputs[a].at[:, cols(core, h)], own.at[h, a, mine], loc_sem.at[h, a])

    def mate_in(h, a):
        return pltpu.make_async_remote_copy(
            src_ref=inputs[a].at[:, cols(1 - core, h)], dst_ref=own.at[h, a, mine],
            send_sem=xs_sem.at[h, a], recv_sem=xr_sem.at[h, a], device_id=mate, device_id_type=MESH)

    def mate_in_arrival(h, a):
        return pltpu.make_async_remote_copy(
            src_ref=own.at[h, a, mates], dst_ref=own.at[h, a, mates],
            send_sem=xs_sem.at[h, a], recv_sem=xr_sem.at[h, a], device_id=mate, device_id_type=MESH)

    def hop(src, dst, h, lo, size, ss, rs, to):
        return pltpu.make_async_remote_copy(
            src_ref=src.at[h, pl.ds(lo, size)], dst_ref=dst.at[h, pl.ds(lo, size)],
            send_sem=ss.at[h], recv_sem=rs.at[h], device_id=to, device_id_type=MESH)

    def keys_a(h):
        return hop(kv_out, kv_in, h, 0, na, kas_sem, kar_sem, ahead)

    def keys_b(h):
        return hop(kv_out, kv_in, h, na, 2, kbs_sem, kbr_sem, ahead)

    def rows_a(h):
        return hop(qg_out, qg_in, h, 0, na, qas_sem, qar_sem, behind)

    def rows_b(h):
        return hop(qg_out, qg_in, h, na, 2, qbs_sem, qbr_sem, behind)

    def stats_near(h):
        return hop(stat_out, stat_near, h, 0, 16, sns_sem, snr_sem, behind)

    def stats_far(h):
        return hop(stat_out, stat_far, h, 0, 16, sfs_sem, sfr_sem, behind_two)

    def local_res(h, a):
        return pltpu.make_async_copy(stage.at[h, a, mine], outputs[a].at[:, cols(core, h)], ol_sem.at[h, a])

    def mate_res(h, a):
        return pltpu.make_async_remote_copy(
            src_ref=stage.at[h, a, mates], dst_ref=outputs[a].at[:, cols(core, h)],
            send_sem=os_sem.at[h, a], recv_sem=or_sem.at[h, a], device_id=mate, device_id_type=MESH)

    def mate_res_arrival(h, a):
        return pltpu.make_async_remote_copy(
            src_ref=stage.at[h, a, mates], dst_ref=outputs[a].at[:, cols(1 - core, h)],
            send_sem=os_sem.at[h, a], recv_sem=or_sem.at[h, a], device_id=mate, device_id_type=MESH)

    def live_count(shard):
        s = jnp.clip(shard, 0, n_all - 1)
        total = jnp.int32(0)
        for b in range(owners.shape[1]):
            total += (owners[s // n_seq, b] == lax.rem(s, n_seq)).astype(jnp.int32)
        return jnp.where(jnp.logical_and(shard >= 0, shard < n_all), total, 0)

    c_m3, c_m2, c_m1, c_e, c_o, c_p2, c_p3, c_p4 = [live_count(even + i) for i in range(-3, 5)]
    own_live = (c_e >= 1, c_e >= 2, c_o >= 1, c_o >= 2)

    def arrivals(passed_count, own_count):
        passed, there = [], []
        for t in range(w):
            by_pass = jnp.bool_(False)
            if t == w - 1:
                by_pass = passed_count >= 1
            elif t == w - 2:
                by_pass = passed_count >= 2
            passed.append(by_pass)
            there.append(jnp.logical_and(jnp.logical_not(by_pass), own_count > t))
        return passed, there

    key_passed, key_own = arrivals(c_m3, c_m1 + c_m2)
    row_passed, row_own = arrivals(c_p4, c_p2 + c_p3)

    def fetch(h, a_list):
        for a in a_list:
            local_in(h, a).start()
            mate_in(h, a).start()

    def fetched(h, a_list):
        for a in a_list:
            local_in(h, a).wait()
            mate_in_arrival(h, a).wait_recv()

    def numbered(t, first_count, first, then):
        if t == 0:
            return jnp.where(first_count >= 1, first(0), then(0))
        if t == 1:
            return jnp.where(first_count >= 2, first(1), jnp.where(first_count >= 1, then(0), then(1)))
        if t == 2:
            return jnp.where(first_count >= 2, then(0), then(1))
        return then(1)

    def own_pick(h, x, t):
        def from_even(i):
            return own[h, x, i * BLK:(i + 1) * BLK, :]

        def from_odd(i):
            return own[h, x, (2 + i) * BLK:(3 + i) * BLK, :]

        if x in (KEY, VAL):
            return numbered(t, c_o, from_odd, from_even)
        return numbered(t, c_e, from_even, from_odd)

    def make_a(h, pair, out):
        for t in range(na):
            for i, x in enumerate(pair):
                out[h, t, i] = own_pick(h, x, t)

    def make_b(h, pair, arrived, out, passed_count):
        for i, x in enumerate(pair):
            first, second = arrived[h, 0, i], arrived[h, 1, i]
            if w - 2 < 4:
                second = jnp.where(passed_count >= 2, second, own_pick(h, x, w - 2))
            if w - 1 < 4:
                first = jnp.where(passed_count >= 1, first, own_pick(h, x, w - 1))
            out[h, w - 2, i] = second
            out[h, w - 1, i] = first

    inv_root = HD ** (-0.5)
    exp_scale = inv_root * math.log2(math.e)
    row_id = lax.broadcasted_iota(jnp.int32, (BLK, SL), 0)
    col_id = lax.broadcasted_iota(jnp.int32, (BLK, SL), 1)
    first_half = lax.broadcasted_iota(jnp.int32, (1, SL), 1) < BLK
    nat, both_last = ((1,), (0,)), ((1,), (1,))

    def block(b):
        return slice(b * BLK, (b + 1) * BLK)

    def query_side(h):
        keys, vals = own[h, KEY], own[h, VAL]
        far_keys = kv_in[h, :, 0].reshape(w * BLK, HD)
        far_vals = kv_in[h, :, 1].reshape(w * BLK, HD)
        prod = own[h, GRD].astype(F32) * own[h, OUT].astype(F32)
        delta_all = jnp.sum(prod.T, axis=0, keepdims=True)
        for a in range(2):
            nk = SL * (a + 1)
            rows = slice(a * SL, (a + 1) * SL)
            query, grad = own[h, QRY, rows], own[h, GRD, rows]
            delta = delta_all[:, rows]
            s_buf[0:nk] = dot(keys[:nk], query, both_last)
            s_buf[2 * SL:] = dot(far_keys, query, both_last)
            dp_buf[0:nk] = dot(vals[:nk], grad, both_last)
            dp_buf[2 * SL:] = dot(far_vals, grad, both_last)
            blocks = list(range(nk // BLK)) + [4 + t for t in range(w)]
            top = None
            for b in blocks:
                if b >= 4:
                    ok = key_own[b - 4]
                    if a == 0:
                        ok = jnp.logical_or(ok, key_passed[b - 4])
                else:
                    ok = own_live[b]
                x = s_buf[block(b)] + jnp.where(ok, 0.0, NEG).astype(F32)
                if b < 4 and b >= 2 * a:
                    x = jnp.where(row_id + (b - 2 * a) * BLK <= col_id, x, NEG)
                s_buf[block(b)] = x
                high = jnp.max(x, axis=0, keepdims=True)
                top = high if top is None else jnp.maximum(top, high)
            total = None
            for b in blocks:
                e = jnp.exp2((s_buf[block(b)] - top) * exp_scale)
                s_buf[block(b)] = e
                part = jnp.sum(e, axis=0, keepdims=True)
                total = part if total is None else total + part
            live = jnp.where(first_half, jnp.where(own_live[2 * a], 1.0, 0.0).astype(F32),
                             jnp.where(own_live[2 * a + 1], 1.0, 0.0).astype(F32))
            scale = live / total
            for i in range(2):
                for r, stat in enumerate((top, scale, delta)):
                    stat_out[h, 4 * r + 2 * a + i:4 * r + 2 * a + i + 1, :] = stat[:, block(i)]
            for b in blocks:
                prob = s_buf[block(b)] * scale
                if b < 4:
                    p_buf[block(b), rows] = prob.astype(BF16)
                ds_buf[block(b), rows] = (prob * (dp_buf[block(b)] - delta)).astype(BF16)
            dq = dot(ds_buf[0:nk, rows], keys[:nk], ((0,), (0,)))
            dq += dot(ds_buf[2 * SL:, rows], far_keys, ((0,), (0,)))
            stage[h, 0, rows] = (dq * inv_root).astype(BF16)

    def own_keys(h):
        second = slice(SL, 2 * SL)
        query, grad = own[h, QRY], own[h, GRD]
        part_own[h, 0, 0:SL] = dot(ds_buf[0:SL], query, nat)
        part_own[h, 0, second] = dot(ds_buf[second, second], query[second], nat)
        part_own[h, 1, 0:SL] = dot(p_buf[0:SL], grad, nat)
        part_own[h, 1, second] = dot(p_buf[second, second], grad[second], nat)

    def key_side(h):
        queries = qg_in[h, :, 0].reshape(w * BLK, HD)
        grads = qg_in[h, :, 1].reshape(w * BLK, HD)
        sk_buf[...] = dot(own[h, KEY], queries, both_last)
        dpk_buf[...] = dot(own[h, VAL], grads, both_last)
        for t in range(w):
            def stat(r):
                def near(i):
                    return stat_near[h, 4 * r + i:4 * r + i + 1, :]

                row = numbered(t, c_p2, near, lambda i: near(2 + i))
                if t == w - 1:
                    row = jnp.where(row_passed[t], stat_far[h, 4 * r:4 * r + 1, :], row)
                if t == w - 2:
                    row = jnp.where(row_passed[t], stat_far[h, 4 * r + 1:4 * r + 2, :], row)
                return row

            top, scale, delta = stat(0), stat(1), stat(2)
            for b in range(4):
                ok = row_own[t]
                if b >= 2:
                    ok = jnp.logical_or(ok, row_passed[t])
                level = jnp.where(jnp.logical_and(ok, own_live[b]), top, -NEG)
                prob = jnp.exp2((sk_buf[block(b), block(t)] - level) * exp_scale) * scale
                pk_buf[block(b), block(t)] = prob.astype(BF16)
                dsk_buf[block(b), block(t)] = (prob * (dpk_buf[block(b), block(t)] - delta)).astype(BF16)
        dk = part_own[h, 0] + dot(dsk_buf[...], queries, nat)
        stage[h, 1] = (dk * inv_root).astype(BF16)
        stage[h, 2] = (part_own[h, 1] + dot(pk_buf[...], grads, nat)).astype(BF16)

    early = min(LEAD, nh)
    for h in range(early):
        for a in (KEY, VAL, QRY, GRD):
            local_in(h, a).start()

    @pl.when(jnp.logical_not(has_behind))
    def _():
        kv_in[...] = jnp.zeros_like(kv_in)

    @pl.when(jnp.logical_not(has_ahead))
    def _():
        qg_in[...] = jnp.zeros_like(qg_in)
        stat_near[...] = jnp.zeros_like(stat_near)

    @pl.when(jnp.logical_not(has_ahead_two))
    def _():
        stat_far[...] = jnp.zeros_like(stat_far)

    pl.semaphore_wait(barrier, met)
    for h in range(early):
        for a in (KEY, VAL, QRY, GRD):
            mate_in(h, a).start()

    def start_a(h):
        fetched(h, (KEY, VAL))

        @when_ahead
        def _():
            make_a(h, (KEY, VAL), kv_out)
            keys_a(h).start()

        fetched(h, (QRY, GRD))

        @when_behind
        def _():
            make_a(h, (QRY, GRD), qg_out)
            rows_a(h).start()

    for h in range(early):
        start_a(h)

    for h in range(early):
        fetch(h, (OUT,))

    @pl.loop(early, nh)
    def _(h):
        fetch(h, (KEY, VAL, QRY, GRD, OUT))

    @pl.loop(0, nh + KEY_LAG)
    def _(step):
        @pl.when(step < nh)
        def _():
            h = step

            @when_behind
            def _():
                keys_a(h).wait_recv()

            @when_ahead
            def _():
                make_b(h, (KEY, VAL), kv_in, kv_out, c_m1)
                keys_b(h).start()
                rows_a(h).wait_recv()

            @when_behind
            def _():
                make_b(h, (QRY, GRD), qg_in, qg_out, c_p2)
                rows_b(h).start()

        @pl.when(step + early < nh)
        def _():
            start_a(step + early)

        @pl.when(step >= KEY_LAG)
        def _():
            h = step - KEY_LAG

            @when_ahead
            def _():
                rows_b(h).wait_recv()
                stats_near(h).wait_recv()

            @when_ahead_two
            def _():
                stats_far(h).wait_recv()

            key_side(h)
            for a in (1, 2):
                local_res(h, a).start()
                mate_res(h, a).start()

        @pl.when(jnp.logical_and(step >= QUERY_LAG, step < nh + QUERY_LAG))
        def _():
            h = step - QUERY_LAG
            fetched(h, (OUT,))

            @when_behind
            def _():
                keys_b(h).wait_recv()

            query_side(h)

            @when_behind
            def _():
                stats_near(h).start()

            @when_behind_two
            def _():
                stats_far(h).start()

            local_res(h, 0).start()
            mate_res(h, 0).start()
            own_keys(h)

    @pl.loop(0, nh)
    def _(h):
        for a in range(5):
            mate_in(h, a).wait_send()

        @when_ahead
        def _():
            keys_a(h).wait_send()
            keys_b(h).wait_send()

        @when_behind
        def _():
            rows_a(h).wait_send()
            rows_b(h).wait_send()
            stats_near(h).wait_send()

        @when_behind_two
        def _():
            stats_far(h).wait_send()

        for a in range(3):
            local_res(h, a).wait()
            mate_res(h, a).wait_send()
            mate_res_arrival(h, a).wait_recv()


def fused(w, owners, queries, key_states, value_states, attn_out, out_grad):
    width = queries.shape[1]
    nh = width // (2 * HD)
    anywhere = pl.BlockSpec(memory_space=pl.ANY)
    dma = pltpu.SemaphoreType.DMA
    slots = pltpu.VMEM((nh, w, 2, BLK, HD), BF16)
    stats = pltpu.VMEM((nh, 16, HD), F32)
    return pl.pallas_call(
        functools.partial(kernel, w, nh),
        out_shape=[jax.ShapeDtypeStruct(queries.shape, BF16)] * 3,
        in_specs=[pl.BlockSpec(memory_space=pltpu.SMEM)] + [anywhere] * 5,
        out_specs=[anywhere] * 3,
        scratch_shapes=[
            pltpu.VMEM((nh, 5, 2 * SL, HD), BF16),
            slots, slots, slots, slots,
            stats, stats, stats,
            pltpu.VMEM((nh, 2, 2 * SL, HD), F32),
            pltpu.VMEM((nh, 3, 2 * SL, HD), BF16),
            pltpu.VMEM(((4 + w) * BLK, SL), F32),
            pltpu.VMEM(((4 + w) * BLK, SL), F32),
            pltpu.VMEM((2 * SL, 2 * SL), BF16),
            pltpu.VMEM(((4 + w) * BLK, 2 * SL), BF16),
            pltpu.VMEM((2 * SL, w * BLK), F32),
            pltpu.VMEM((2 * SL, w * BLK), F32),
            pltpu.VMEM((2 * SL, w * BLK), BF16),
            pltpu.VMEM((2 * SL, w * BLK), BF16),
            dma((nh, 5)), dma((nh, 5)), dma((nh, 5)),
        ] + [dma((nh,))] * 12 + [dma((nh, 3))] * 3,
        compiler_params=pltpu.CompilerParams(
            collective_id=w - 4, has_side_effects=True, vmem_limit_bytes=56 * 2**20),
        name="slots%d" % w,
    )(owners, queries, key_states, value_states, attn_out, out_grad)


def place(a, b, c, x, y, z, sems):
    copies = [pltpu.make_async_copy(s, d, sems.at[i]) for i, (s, d) in enumerate(((a, x), (b, y), (c, z)))]
    for copy in copies:
        copy.start()
    for copy in copies:
        copy.wait()


def placed(arrays):
    anywhere = pl.BlockSpec(memory_space=pl.ANY)
    return pl.pallas_call(
        place, out_shape=[jax.ShapeDtypeStruct(a.shape, a.dtype) for a in arrays],
        in_specs=[anywhere] * 3, out_specs=[anywhere] * 3,
        scratch_shapes=[pltpu.SemaphoreType.DMA((3,))], name="place")(*arrays)


def per_device(queries, key_states, value_states, attn_out, out_grad, owner_ids):
    n_grp, n_seq = lax.axis_size("grp"), lax.axis_size("seq")
    shard = (owner_ids + n_seq * jnp.arange(n_grp, dtype=jnp.int32)[:, None]).reshape(-1)
    last = shard + 2 - jnp.logical_or(shard == 0, shard == n_grp * n_seq - 3).astype(jnp.int32)
    five = (shard[4:] <= last[:-4]).astype(jnp.int32)
    six = (jnp.pad(shard[5:], (0, 1), constant_values=n_grp * n_seq + 2) <= last[:-4]).astype(jnp.int32)
    return placed(lax.switch(
        jnp.max(five + six),
        [functools.partial(fused, w) for w in (4, 5, 6)],
        owner_ids, queries, key_states, value_states, attn_out, out_grad))


def solution(mesh):
    rows = P(("grp", "seq"), None)
    return jax.shard_map(
        per_device,
        mesh=mesh,
        in_specs=(rows,) * 5 + (P(),),
        out_specs=(rows,) * 3,
        check_vma=False,
    )
```

```python
import functools
import math

import jax
import jax.numpy as jnp
from jax import lax
from jax.experimental import pallas as pl
from jax.experimental.pallas import tpu as pltpu
from jax.sharding import PartitionSpec as P

HD = 128
BLK = 128
SL = 256
MESH = pl.DeviceIdType.MESH
F32 = jnp.float32
BF16 = jnp.bfloat16
NEG = -1e30
LEAD, QUERY_LAG, KEY_LAG, DRAIN_LAG = 2, 1, 3, 5
KEY, VAL, QRY, GRD, OUT = range(5)


def dot(a, b, dims):
    return lax.dot_general(a, b, (dims, ((), ())), preferred_element_type=F32)


def needs(far, first, second, next_one, next_two, next_three):
    near_two = next_one + next_two
    return (jnp.where(next_one > 0, far, 0), jnp.where(near_two > 0, first, 0),
            jnp.where(near_two + next_three > 0, second, 0))


def kernel(w, nh, owners_in, q_in, k_in, v_in, o_in, g_in, dq_out, dk_out, dv_out,
           own, kv_out, kv_in, qg_out, qg_in, stat_out, stat_near, stat_far, part_own, stage,
           s_buf, dp_buf, p_buf, ds_buf, sk_buf, dpk_buf, pk_buf, dsk_buf,
           owners, owners_sem, loc_sem, xs_sem, xr_sem, kas_sem, kar_sem, kbs_sem, kbr_sem, qas_sem, qar_sem, qbs_sem, qbr_sem,
           sns_sem, snr_sem, sfs_sem, sfr_sem, ol_sem, os_sem, or_sem):
    n_seq = lax.axis_size("seq")
    n_all = lax.axis_size("grp") * n_seq
    me = lax.axis_index("grp") * n_seq + lax.axis_index("seq")
    core = lax.rem(me, 2)
    even = me - core
    na = w - 2

    def dev(d):
        d = lax.rem(d + n_all, n_all)
        return (d // n_seq, lax.rem(d, n_seq))

    def only(cond):
        return lambda act: pl.when(cond)(act)

    mate = dev(even + 1 - core)
    ahead, ahead_two, behind, behind_two = [dev(me + i) for i in (2, 4, -2, -4)]
    has_ahead, has_ahead_two = me < n_all - 2, me < n_all - 4
    has_behind, has_behind_two = me >= 2, me >= 4
    when_ahead, when_ahead_two = only(has_ahead), only(has_ahead_two)
    when_behind, when_behind_two = only(has_behind), only(has_behind_two)

    barrier = pltpu.get_barrier_semaphore()
    pl.semaphore_signal(barrier, inc=1, device_id=mate, device_id_type=MESH)
    met = jnp.int32(1)
    for there, other in ((has_ahead, ahead), (has_behind, behind), (has_ahead_two, ahead_two), (has_behind_two, behind_two)):
        @pl.when(there)
        def _():
            pl.semaphore_signal(barrier, inc=1, device_id=other, device_id_type=MESH)

        met += there.astype(jnp.int32)

    owners_copy = pltpu.make_async_copy(owners_in, owners, owners_sem)
    owners_copy.start()

    inputs = (k_in, v_in, q_in, g_in, o_in)
    outputs = (dq_out, dk_out, dv_out)

    def cols(which_core, h):
        return pl.ds(pl.multiple_of((which_core * nh + h) * HD, HD), HD)

    mine = pl.ds(pl.multiple_of(core * SL, SL), SL)
    mates = pl.ds(pl.multiple_of((1 - core) * SL, SL), SL)

    def local_in(h, a):
        return pltpu.make_async_copy(inputs[a].at[:, cols(core, h)], own.at[h, a, mine], loc_sem.at[h, a])

    def mate_in(h, a):
        return pltpu.make_async_remote_copy(
            src_ref=inputs[a].at[:, cols(1 - core, h)], dst_ref=own.at[h, a, mine],
            send_sem=xs_sem.at[h, a], recv_sem=xr_sem.at[h, a], device_id=mate, device_id_type=MESH)

    def mate_in_arrival(h, a):
        return pltpu.make_async_remote_copy(
            src_ref=own.at[h, a, mates], dst_ref=own.at[h, a, mates],
            send_sem=xs_sem.at[h, a], recv_sem=xr_sem.at[h, a], device_id=mate, device_id_type=MESH)

    def hop(src, dst, h, lo, size, ss, rs, to):
        return pltpu.make_async_remote_copy(
            src_ref=src.at[h, pl.ds(lo, size)], dst_ref=dst.at[h, pl.ds(lo, size)],
            send_sem=ss.at[h], recv_sem=rs.at[h], device_id=to, device_id_type=MESH)

    def keys_a(h):
        return hop(kv_out, kv_in, h, 0, na, kas_sem, kar_sem, ahead)

    def keys_b(h, i):
        return pltpu.make_async_remote_copy(
            src_ref=kv_out.at[h, pl.ds(na, 2), i], dst_ref=kv_in.at[h, pl.ds(na, 2), i],
            send_sem=kbs_sem.at[h, i], recv_sem=kbr_sem.at[h, i], device_id=ahead, device_id_type=MESH)

    def rows_a(h):
        return hop(qg_out, qg_in, h, 0, na, qas_sem, qar_sem, behind)

    def rows_b(h):
        return hop(qg_out, qg_in, h, na, 2, qbs_sem, qbr_sem, behind)

    def stats_near(h):
        return hop(stat_out, stat_near, h, 0, 16, sns_sem, snr_sem, behind)

    def stats_far(h):
        return hop(stat_out, stat_far, h, 0, 16, sfs_sem, sfr_sem, behind_two)

    def local_res(h, a):
        return pltpu.make_async_copy(stage.at[h, a, mine], outputs[a].at[:, cols(core, h)], ol_sem.at[h, a])

    def mate_res(h, a):
        return pltpu.make_async_remote_copy(
            src_ref=stage.at[h, a, mates], dst_ref=outputs[a].at[:, cols(core, h)],
            send_sem=os_sem.at[h, a], recv_sem=or_sem.at[h, a], device_id=mate, device_id_type=MESH)

    def mate_res_arrival(h, a):
        return pltpu.make_async_remote_copy(
            src_ref=stage.at[h, a, mates], dst_ref=outputs[a].at[:, cols(1 - core, h)],
            send_sem=os_sem.at[h, a], recv_sem=or_sem.at[h, a], device_id=mate, device_id_type=MESH)

    def give(h, a):
        local_res(h, a).start()
        mate_res(h, a).start()

    def live_count(shard):
        s = jnp.clip(shard, 0, n_all - 1)
        total = jnp.int32(0)
        for b in range(owners.shape[1]):
            total += (owners[s // n_seq, b] == lax.rem(s, n_seq)).astype(jnp.int32)
        return jnp.where(jnp.logical_and(shard >= 0, shard < n_all), total, 0)

    early = min(LEAD, nh)
    for h in range(early):
        for a in (KEY, VAL, QRY, GRD):
            local_in(h, a).start()

    owners_copy.wait()
    m3, m2, m1, e0, o0, p2, p3, p4 = [live_count(even + i) for i in range(-3, 5)]
    own_live = (e0 >= 1, e0 >= 2, o0 >= 1, o0 >= 2)

    key_from_far, key_from_even, key_from_odd = needs(m3, m2, m1, e0, o0, p2)
    key_pass, key_even, key_odd = needs(m1, e0, o0, p2, p3, p4)
    row_from_far, row_from_odd, row_from_even = needs(p4, p3, p2, o0, e0, m1)
    row_pass, row_odd, row_even = needs(p2, o0, e0, m1, m2, m3)

    def arrivals(passed_count, own_count):
        passed, there = [], []
        for t in range(w):
            by_pass = jnp.bool_(False)
            if t == w - 1:
                by_pass = passed_count >= 1
            elif t == w - 2:
                by_pass = passed_count >= 2
            passed.append(by_pass)
            there.append(jnp.logical_and(jnp.logical_not(by_pass), own_count > t))
        return passed, there

    key_passed, key_own = arrivals(key_from_far, key_from_even + key_from_odd)
    row_passed, row_own = arrivals(row_from_far, row_from_even + row_from_odd)

    def fetch(h, a_list):
        for a in a_list:
            local_in(h, a).start()
            mate_in(h, a).start()

    def fetched(h, a_list):
        for a in a_list:
            local_in(h, a).wait()
            mate_in_arrival(h, a).wait_recv()

    def numbered(t, first_count, first, then):
        if t == 0:
            return jnp.where(first_count >= 1, first(0), then(0))
        if t == 1:
            return jnp.where(first_count >= 2, first(1), jnp.where(first_count >= 1, then(0), then(1)))
        if t == 2:
            return jnp.where(first_count >= 2, then(0), then(1))
        return then(1)

    def own_pick(h, x, t):
        def from_even(i):
            return own[h, x, i * BLK:(i + 1) * BLK, :]

        def from_odd(i):
            return own[h, x, (2 + i) * BLK:(3 + i) * BLK, :]

        if x in (KEY, VAL):
            return numbered(t, key_odd, from_odd, from_even)
        return numbered(t, row_even, from_even, from_odd)

    def make_a(h, pair, out):
        for t in range(na):
            for i, x in enumerate(pair):
                out[h, t, i] = own_pick(h, x, t)

    def make_b(h, pair, arrived, out, passed_count):
        for i, x in enumerate(pair):
            first, second = arrived[h, 0, i], arrived[h, 1, i]
            if w - 2 < 4:
                second = jnp.where(passed_count >= 2, second, own_pick(h, x, w - 2))
            if w - 1 < 4:
                first = jnp.where(passed_count >= 1, first, own_pick(h, x, w - 1))
            out[h, w - 2, i] = second
            out[h, w - 1, i] = first

    inv_root = HD ** (-0.5)
    exp_scale = inv_root * math.log2(math.e)
    row_id = lax.broadcasted_iota(jnp.int32, (BLK, SL), 0)
    col_id = lax.broadcasted_iota(jnp.int32, (BLK, SL), 1)
    first_half = lax.broadcasted_iota(jnp.int32, (1, SL), 1) < BLK
    nat, both_last = ((1,), (0,)), ((1,), (1,))

    def block(b):
        return slice(b * BLK, (b + 1) * BLK)

    def half(a):
        return 2 * (a + 1), slice(a * SL, (a + 1) * SL)

    def soft_part(h):
        keys = own[h, KEY]
        far_keys = kv_in[h, :, 0].reshape(w * BLK, HD)
        prod = own[h, GRD].astype(F32) * own[h, OUT].astype(F32)
        delta_all = jnp.sum(prod.T, axis=0, keepdims=True)
        for a in range(2):
            near, rows = half(a)
            query = own[h, QRY, rows]
            s_buf[0:near * BLK, rows] = dot(keys[:near * BLK], query, both_last)
            s_buf[4 * BLK:, rows] = dot(far_keys, query, both_last)
        for a in range(2):
            near, rows = half(a)
            blocks = list(range(near)) + [4 + t for t in range(w)]
            top = None
            for b in blocks:
                if b >= 4:
                    ok = key_own[b - 4]
                    if a == 0:
                        ok = jnp.logical_or(ok, key_passed[b - 4])
                else:
                    ok = own_live[b]
                x = s_buf[block(b), rows] + jnp.where(ok, 0.0, NEG).astype(F32)
                if b < 4 and b >= 2 * a:
                    x = jnp.where(row_id + (b - 2 * a) * BLK <= col_id, x, NEG)
                s_buf[block(b), rows] = x
                high = jnp.max(x, axis=0, keepdims=True)
                top = high if top is None else jnp.maximum(top, high)
            total = None
            for b in blocks:
                e = jnp.exp2((s_buf[block(b), rows] - top) * exp_scale)
                s_buf[block(b), rows] = e
                part = jnp.sum(e, axis=0, keepdims=True)
                total = part if total is None else total + part
            live = jnp.where(first_half, jnp.where(own_live[2 * a], 1.0, 0.0).astype(F32),
                             jnp.where(own_live[2 * a + 1], 1.0, 0.0).astype(F32))
            for r, stat in enumerate((top, live / total, delta_all[:, rows])):
                for i in range(2):
                    at = 4 * r + 2 * a + i
                    stat_out[h, at:at + 1, :] = stat[:, block(i)]

    def grad_part(h):
        keys, vals = own[h, KEY], own[h, VAL]
        far_keys = kv_in[h, :, 0].reshape(w * BLK, HD)
        far_vals = kv_in[h, :, 1].reshape(w * BLK, HD)
        for a in range(2):
            near, rows = half(a)
            grad = own[h, GRD, rows]
            dp_buf[0:near * BLK] = dot(vals[:near * BLK], grad, both_last)
            dp_buf[4 * BLK:] = dot(far_vals, grad, both_last)
            scale, delta = [
                jnp.concatenate([stat_out[h, at:at + 1, :] for at in (4 * r + 2 * a, 4 * r + 2 * a + 1)], axis=1)
                for r in (1, 2)]
            for b in list(range(near)) + [4 + t for t in range(w)]:
                prob = s_buf[block(b), rows] * scale
                if b < 4:
                    p_buf[block(b), rows] = prob.astype(BF16)
                ds_buf[block(b), rows] = (prob * (dp_buf[block(b)] - delta)).astype(BF16)
            dq = dot(ds_buf[0:near * BLK, rows], keys[:near * BLK], ((0,), (0,)))
            dq += dot(ds_buf[4 * BLK:, rows], far_keys, ((0,), (0,)))
            stage[h, 0, rows] = (dq * inv_root).astype(BF16)

    def own_keys(h):
        second = slice(SL, 2 * SL)
        query, grad = own[h, QRY], own[h, GRD]
        part_own[h, 0, 0:SL] = dot(ds_buf[0:SL], query, nat)
        part_own[h, 0, second] = dot(ds_buf[second, second], query[second], nat)
        part_own[h, 1, 0:SL] = dot(p_buf[0:SL], grad, nat)
        part_own[h, 1, second] = dot(p_buf[second, second], grad[second], nat)

    def key_side(h):
        queries = qg_in[h, :, 0].reshape(w * BLK, HD)
        grads = qg_in[h, :, 1].reshape(w * BLK, HD)
        sk_buf[...] = dot(own[h, KEY], queries, both_last)
        dpk_buf[...] = dot(own[h, VAL], grads, both_last)
        for t in range(w):
            def stat(r):
                def near(i):
                    return stat_near[h, 4 * r + i:4 * r + i + 1, :]

                row = numbered(t, row_from_even, near, lambda i: near(2 + i))
                if t == w - 1:
                    row = jnp.where(row_passed[t], stat_far[h, 4 * r:4 * r + 1, :], row)
                if t == w - 2:
                    row = jnp.where(row_passed[t], stat_far[h, 4 * r + 1:4 * r + 2, :], row)
                return row

            top, scale, delta = stat(0), stat(1), stat(2)
            for b in range(4):
                ok = row_own[t]
                if b >= 2:
                    ok = jnp.logical_or(ok, row_passed[t])
                level = jnp.where(jnp.logical_and(ok, own_live[b]), top, -NEG)
                prob = jnp.exp2((sk_buf[block(b), block(t)] - level) * exp_scale) * scale
                pk_buf[block(b), block(t)] = prob.astype(BF16)
                dsk_buf[block(b), block(t)] = (prob * (dpk_buf[block(b), block(t)] - delta)).astype(BF16)
        stage[h, 2] = (part_own[h, 1] + dot(pk_buf[...], grads, nat)).astype(BF16)
        give(h, 2)
        dk = part_own[h, 0] + dot(dsk_buf[...], queries, nat)
        stage[h, 1] = (dk * inv_root).astype(BF16)
        give(h, 1)

    @pl.when(jnp.logical_not(has_behind))
    def _():
        kv_in[...] = jnp.zeros_like(kv_in)

    @pl.when(jnp.logical_not(has_ahead))
    def _():
        qg_in[...] = jnp.zeros_like(qg_in)
        stat_near[...] = jnp.zeros_like(stat_near)

    @pl.when(jnp.logical_not(has_ahead_two))
    def _():
        stat_far[...] = jnp.zeros_like(stat_far)

    pl.semaphore_wait(barrier, met)
    for h in range(early):
        for a in (KEY, VAL, QRY, GRD):
            mate_in(h, a).start()

    def start_keys(h):
        fetched(h, (KEY, VAL))

        @when_ahead
        def _():
            make_a(h, (KEY, VAL), kv_out)
            keys_a(h).start()

    def start_rows(h):
        fetched(h, (QRY, GRD))

        @when_behind
        def _():
            make_a(h, (QRY, GRD), qg_out)
            rows_a(h).start()

    for h in range(early):
        start_keys(h)
        start_rows(h)

    for h in range(early):
        fetch(h, (OUT,))

    @pl.loop(early, nh)
    def _(h):
        fetch(h, (KEY, VAL, QRY, GRD, OUT))

    def drain(h):
        for a in range(5):
            mate_in(h, a).wait_send()

        @when_ahead
        def _():
            keys_a(h).wait_send()
            for i in range(2):
                keys_b(h, i).wait_send()

        @when_behind
        def _():
            rows_a(h).wait_send()
            rows_b(h).wait_send()
            stats_near(h).wait_send()

        @when_behind_two
        def _():
            stats_far(h).wait_send()

        for a in range(3):
            local_res(h, a).wait()
            mate_res(h, a).wait_send()
            mate_res_arrival(h, a).wait_recv()

    @pl.loop(0, nh + DRAIN_LAG)
    def _(step):
        @pl.when(step < nh)
        def _():
            h = step

            @when_behind
            def _():
                keys_a(h).wait_recv()

            @when_ahead
            def _():
                make_b(h, (KEY, VAL), kv_in, kv_out, key_pass)
                for i in range(2):
                    keys_b(h, i).start()

        @pl.when(step + early < nh)
        def _():
            start_keys(step + early)

        @pl.when(step < nh)
        def _():
            h = step

            @when_ahead
            def _():
                rows_a(h).wait_recv()

            @when_behind
            def _():
                make_b(h, (QRY, GRD), qg_in, qg_out, row_pass)
                rows_b(h).start()

        @pl.when(step + early < nh)
        def _():
            start_rows(step + early)

        @pl.when(jnp.logical_and(step >= KEY_LAG, step < nh + KEY_LAG))
        def _():
            h = step - KEY_LAG

            @when_ahead
            def _():
                rows_b(h).wait_recv()
                stats_near(h).wait_recv()

            @when_ahead_two
            def _():
                stats_far(h).wait_recv()

            key_side(h)

        @pl.when(jnp.logical_and(step >= QUERY_LAG, step < nh + QUERY_LAG))
        def _():
            h = step - QUERY_LAG
            fetched(h, (OUT,))

            @when_behind
            def _():
                keys_b(h, 0).wait_recv()

            soft_part(h)

            @when_behind
            def _():
                stats_near(h).start()

            @when_behind_two
            def _():
                stats_far(h).start()

            @when_behind
            def _():
                keys_b(h, 1).wait_recv()

            grad_part(h)
            give(h, 0)
            own_keys(h)

        @pl.when(step >= DRAIN_LAG)
        def _():
            drain(step - DRAIN_LAG)


def fused(w, owners, queries, key_states, value_states, attn_out, out_grad):
    width = queries.shape[1]
    nh = width // (2 * HD)
    anywhere = pl.BlockSpec(memory_space=pl.ANY)
    dma = pltpu.SemaphoreType.DMA
    slots = pltpu.VMEM((nh, w, 2, BLK, HD), BF16)
    stats = pltpu.VMEM((nh, 16, HD), F32)
    return pl.pallas_call(
        functools.partial(kernel, w, nh),
        out_shape=[jax.ShapeDtypeStruct(queries.shape, BF16)] * 3,
        in_specs=[anywhere] * 6,
        out_specs=[anywhere] * 3,
        scratch_shapes=[
            pltpu.VMEM((nh, 5, 2 * SL, HD), BF16),
            slots, slots, slots, slots,
            stats, stats, stats,
            pltpu.VMEM((nh, 2, 2 * SL, HD), F32),
            pltpu.VMEM((nh, 3, 2 * SL, HD), BF16),
            pltpu.VMEM(((4 + w) * BLK, 2 * SL), F32),
            pltpu.VMEM(((4 + w) * BLK, SL), F32),
            pltpu.VMEM((2 * SL, 2 * SL), BF16),
            pltpu.VMEM(((4 + w) * BLK, 2 * SL), BF16),
            pltpu.VMEM((2 * SL, w * BLK), F32),
            pltpu.VMEM((2 * SL, w * BLK), F32),
            pltpu.VMEM((2 * SL, w * BLK), BF16),
            pltpu.VMEM((2 * SL, w * BLK), BF16),
            pltpu.SMEM(owners.shape, jnp.int32), dma,
            dma((nh, 5)), dma((nh, 5)), dma((nh, 5)),
            dma((nh,)), dma((nh,)), dma((nh, 2)), dma((nh, 2)),
        ] + [dma((nh,))] * 8 + [dma((nh, 3))] * 3,
        compiler_params=pltpu.CompilerParams(
            collective_id=w - 4, has_side_effects=True, vmem_limit_bytes=56 * 2**20),
        name="slots%d" % w,
    )(owners, queries, key_states, value_states, attn_out, out_grad)


def place(a, b, c, x, y, z, sems):
    copies = [pltpu.make_async_copy(s, d, sems.at[i]) for i, (s, d) in enumerate(((a, x), (b, y), (c, z)))]
    for copy in copies:
        copy.start()
    for copy in copies:
        copy.wait()


def placed(arrays):
    anywhere = pl.BlockSpec(memory_space=pl.ANY)
    return pl.pallas_call(
        place, out_shape=[jax.ShapeDtypeStruct(a.shape, a.dtype) for a in arrays],
        in_specs=[anywhere] * 3, out_specs=[anywhere] * 3,
        scratch_shapes=[pltpu.SemaphoreType.DMA((3,))], name="place")(*arrays)


def per_device(queries, key_states, value_states, attn_out, out_grad, owner_ids):
    n_grp, n_seq = lax.axis_size("grp"), lax.axis_size("seq")
    shard = (owner_ids + n_seq * jnp.arange(n_grp, dtype=jnp.int32)[:, None]).reshape(-1, 1, 1)
    chip = jnp.arange(n_grp * n_seq // 2, dtype=jnp.int32)[None, :]
    around = 2 * chip + jnp.arange(-3, 5, dtype=jnp.int32)[:, None]
    m3, m2, m1, e0, o0, p2, p3, p4 = jnp.sum((shard == around).astype(jnp.int32), axis=0)
    most = jnp.max(jnp.maximum(sum(needs(m1, e0, o0, p2, p3, p4)), sum(needs(p2, o0, e0, m1, m2, m3))))
    return placed(lax.switch(
        most - 4,
        [functools.partial(fused, w) for w in (4, 5, 6)],
        owner_ids, queries, key_states, value_states, attn_out, out_grad))


def solution(mesh):
    rows = P(("grp", "seq"), None)
    return jax.shard_map(
        per_device,
        mesh=mesh,
        in_specs=(rows,) * 5 + (P(),),
        out_specs=(rows,) * 3,
        check_vma=False,
    )
```

```python
import functools
import math

import jax
import jax.numpy as jnp
from jax import lax
from jax.experimental import pallas as pl
from jax.experimental.pallas import tpu as pltpu
from jax.sharding import PartitionSpec as P

HD = 128
BLK = 128
SL = 256
MESH = pl.DeviceIdType.MESH
F32 = jnp.float32
BF16 = jnp.bfloat16
NEG = -1e30
LEAD, QUERY_LAG, KEY_LAG, DRAIN_LAG = 2, 1, 3, 5
KEY, VAL, QRY, GRD, OUT = range(5)


def dot(a, b, dims):
    return lax.dot_general(a, b, (dims, ((), ())), preferred_element_type=F32)


def needs(far, first, second, next_one, next_two, next_three):
    near_two = next_one + next_two
    return (jnp.where(next_one > 0, far, 0), jnp.where(near_two > 0, first, 0),
            jnp.where(near_two + next_three > 0, second, 0))


def kernel(w, nh, owners_in, q_in, k_in, v_in, o_in, g_in, dq_out, dk_out, dv_out,
           own, kv_out, kv_in, qg_out, qg_in, stat_out, stat_near, stat_even, stat_far, stat_own, part_own, stage,
           s_buf, dp_buf, p_buf, ds_buf, sk_buf, dpk_buf, pk_buf, dsk_buf,
           owners, owners_sem, loc_sem, xs_sem, xr_sem, kas_sem, kar_sem, kbs_sem, kbr_sem, qas_sem, qar_sem, qbs_sem, qbr_sem,
           sns_sem, snr_sem, sfs_sem, sfr_sem, ol_sem, os_sem, or_sem):
    n_seq = lax.axis_size("seq")
    n_all = lax.axis_size("grp") * n_seq
    me = lax.axis_index("grp") * n_seq + lax.axis_index("seq")
    core = lax.rem(me, 2)
    even = me - core
    na = w - 2

    def dev(d):
        d = lax.rem(d + n_all, n_all)
        return (d // n_seq, lax.rem(d, n_seq))

    def only(cond):
        return lambda act: pl.when(cond)(act)

    mate = dev(even + 1 - core)
    ahead, ahead_two, behind, behind_two = [dev(me + i) for i in (2, 4, -2, -4)]
    has_ahead, has_ahead_two = me < n_all - 2, me < n_all - 4
    has_behind, has_behind_two = me >= 2, me >= 4
    when_ahead, when_ahead_two = only(has_ahead), only(has_ahead_two)
    when_behind, when_behind_two = only(has_behind), only(has_behind_two)

    barrier = pltpu.get_barrier_semaphore()
    pl.semaphore_signal(barrier, inc=1, device_id=mate, device_id_type=MESH)
    met = jnp.int32(1)
    for there, other in ((has_ahead, ahead), (has_behind, behind), (has_ahead_two, ahead_two), (has_behind_two, behind_two)):
        @pl.when(there)
        def _():
            pl.semaphore_signal(barrier, inc=1, device_id=other, device_id_type=MESH)

        met += there.astype(jnp.int32)

    owners_copy = pltpu.make_async_copy(owners_in, owners, owners_sem)
    owners_copy.start()

    inputs = (k_in, v_in, q_in, g_in, o_in)
    outputs = (dq_out, dk_out, dv_out)

    def cols(which_core, h):
        return pl.ds(pl.multiple_of((which_core * nh + h) * HD, HD), HD)

    mine = pl.ds(pl.multiple_of(core * SL, SL), SL)
    mates = pl.ds(pl.multiple_of((1 - core) * SL, SL), SL)

    def local_in(h, a):
        return pltpu.make_async_copy(inputs[a].at[:, cols(core, h)], own.at[h, a, mine], loc_sem.at[h, a])

    def mate_in(h, a):
        return pltpu.make_async_remote_copy(
            src_ref=inputs[a].at[:, cols(1 - core, h)], dst_ref=own.at[h, a, mine],
            send_sem=xs_sem.at[h, a], recv_sem=xr_sem.at[h, a], device_id=mate, device_id_type=MESH)

    def mate_in_arrival(h, a):
        return pltpu.make_async_remote_copy(
            src_ref=own.at[h, a, mates], dst_ref=own.at[h, a, mates],
            send_sem=xs_sem.at[h, a], recv_sem=xr_sem.at[h, a], device_id=mate, device_id_type=MESH)

    def hop(src, dst, h, lo, size, ss, rs, to):
        return pltpu.make_async_remote_copy(
            src_ref=src.at[h, pl.ds(lo, size)], dst_ref=dst.at[h, pl.ds(lo, size)],
            send_sem=ss.at[h], recv_sem=rs.at[h], device_id=to, device_id_type=MESH)

    def keys_a(h):
        return hop(kv_out, kv_in, h, 0, na, kas_sem, kar_sem, ahead)

    def keys_b(h, i):
        return pltpu.make_async_remote_copy(
            src_ref=kv_out.at[h, pl.ds(na, 2), i], dst_ref=kv_in.at[h, pl.ds(na, 2), i],
            send_sem=kbs_sem.at[h, i], recv_sem=kbr_sem.at[h, i], device_id=ahead, device_id_type=MESH)

    def rows_a(h):
        return hop(qg_out, qg_in, h, 0, na, qas_sem, qar_sem, behind)

    def rows_b(h):
        return hop(qg_out, qg_in, h, na, 2, qbs_sem, qbr_sem, behind)

    def stats_near(h):
        return hop(stat_out, stat_near, h, 0, 8, sns_sem, snr_sem, behind)

    def stats_far(h):
        return hop(stat_even, stat_far, h, 0, 4, sfs_sem, sfr_sem, behind_two)

    def local_res(h, a):
        return pltpu.make_async_copy(stage.at[h, a, mine], outputs[a].at[:, cols(core, h)], ol_sem.at[h, a])

    def mate_res(h, a):
        return pltpu.make_async_remote_copy(
            src_ref=stage.at[h, a, mates], dst_ref=outputs[a].at[:, cols(core, h)],
            send_sem=os_sem.at[h, a], recv_sem=or_sem.at[h, a], device_id=mate, device_id_type=MESH)

    def mate_res_arrival(h, a):
        return pltpu.make_async_remote_copy(
            src_ref=stage.at[h, a, mates], dst_ref=outputs[a].at[:, cols(1 - core, h)],
            send_sem=os_sem.at[h, a], recv_sem=or_sem.at[h, a], device_id=mate, device_id_type=MESH)

    def give(h, a):
        local_res(h, a).start()
        mate_res(h, a).start()

    def live_count(shard):
        s = jnp.clip(shard, 0, n_all - 1)
        total = jnp.int32(0)
        for b in range(owners.shape[1]):
            total += (owners[s // n_seq, b] == lax.rem(s, n_seq)).astype(jnp.int32)
        return jnp.where(jnp.logical_and(shard >= 0, shard < n_all), total, 0)

    early = min(LEAD, nh)
    for h in range(early):
        for a in (KEY, VAL, QRY, GRD):
            local_in(h, a).start()

    owners_copy.wait()
    m3, m2, m1, e0, o0, p2, p3, p4 = [live_count(even + i) for i in range(-3, 5)]
    own_live = (e0 >= 1, e0 >= 2, o0 >= 1, o0 >= 2)

    key_from_far, key_from_even, key_from_odd = needs(m3, m2, m1, e0, o0, p2)
    key_pass, key_even, key_odd = needs(m1, e0, o0, p2, p3, p4)
    row_from_far, row_from_odd, row_from_even = needs(p4, p3, p2, o0, e0, m1)
    row_pass, row_odd, row_even = needs(p2, o0, e0, m1, m2, m3)

    def arrivals(passed_count, own_count):
        passed, there = [], []
        for t in range(w):
            by_pass = jnp.bool_(False)
            if t == w - 1:
                by_pass = passed_count >= 1
            elif t == w - 2:
                by_pass = passed_count >= 2
            passed.append(by_pass)
            there.append(jnp.logical_and(jnp.logical_not(by_pass), own_count > t))
        return passed, there

    key_passed, key_own = arrivals(key_from_far, key_from_even + key_from_odd)
    row_passed, row_own = arrivals(row_from_far, row_from_even + row_from_odd)

    def fetch(h, a_list):
        for a in a_list:
            local_in(h, a).start()
            mate_in(h, a).start()

    def fetched(h, a_list):
        for a in a_list:
            local_in(h, a).wait()
            mate_in_arrival(h, a).wait_recv()

    def numbered(t, first_count, first, then):
        if t == 0:
            return jnp.where(first_count >= 1, first(0), then(0))
        if t == 1:
            return jnp.where(first_count >= 2, first(1), jnp.where(first_count >= 1, then(0), then(1)))
        if t == 2:
            return jnp.where(first_count >= 2, then(0), then(1))
        return then(1)

    def own_pick(h, x, t):
        def from_even(i):
            return own[h, x, i * BLK:(i + 1) * BLK, :]

        def from_odd(i):
            return own[h, x, (2 + i) * BLK:(3 + i) * BLK, :]

        if x in (KEY, VAL):
            return numbered(t, key_odd, from_odd, from_even)
        return numbered(t, row_even, from_even, from_odd)

    def make_a(h, pair, out):
        for t in range(na):
            for i, x in enumerate(pair):
                out[h, t, i] = own_pick(h, x, t)

    def make_b(h, pair, arrived, out, passed_count):
        for i, x in enumerate(pair):
            first, second = arrived[h, 0, i], arrived[h, 1, i]
            if w - 2 < 4:
                second = jnp.where(passed_count >= 2, second, own_pick(h, x, w - 2))
            if w - 1 < 4:
                first = jnp.where(passed_count >= 1, first, own_pick(h, x, w - 1))
            out[h, w - 2, i] = second
            out[h, w - 1, i] = first

    inv_root = HD ** (-0.5)
    exp_scale = inv_root * math.log2(math.e)
    row_id = lax.broadcasted_iota(jnp.int32, (BLK, SL), 0)
    col_id = lax.broadcasted_iota(jnp.int32, (BLK, SL), 1)
    first_half = lax.broadcasted_iota(jnp.int32, (1, SL), 1) < BLK
    nat, both_last = ((1,), (0,)), ((1,), (1,))

    def block(b):
        return slice(b * BLK, (b + 1) * BLK)

    def half(a):
        return 2 * (a + 1), slice(a * SL, (a + 1) * SL)

    def soft_part(h):
        keys = own[h, KEY]
        far_keys = kv_in[h, :, 0].reshape(w * BLK, HD)
        prod = own[h, GRD].astype(F32) * own[h, OUT].astype(F32)
        delta_all = jnp.sum(prod.T, axis=0, keepdims=True)
        for a in range(2):
            near, rows = half(a)
            query = own[h, QRY, rows]
            s_buf[0:near * BLK, rows] = dot(keys[:near * BLK], query, both_last)
            s_buf[4 * BLK:, rows] = dot(far_keys, query, both_last)
        for a in range(2):
            near, rows = half(a)
            blocks = list(range(near)) + [4 + t for t in range(w)]
            allowed = []
            for b in blocks:
                ok = own_live[b] if b < 4 else key_own[b - 4]
                if b >= 4 and a == 0:
                    ok = jnp.logical_or(ok, key_passed[b - 4])
                allowed.append(ok)
            top = None
            for b, ok in zip(blocks, allowed):
                x = s_buf[block(b), rows]
                if b < 4 and b >= 2 * a:
                    x = jnp.where(row_id + (b - 2 * a) * BLK <= col_id, x, NEG)
                    s_buf[block(b), rows] = x
                high = jnp.max(x, axis=0, keepdims=True) + jnp.where(ok, 0.0, NEG).astype(F32)
                top = high if top is None else jnp.maximum(top, high)
            total = None
            for b, ok in zip(blocks, allowed):
                e = jnp.exp2((s_buf[block(b), rows] - jnp.where(ok, top, -NEG)) * exp_scale)
                s_buf[block(b), rows] = e
                part = jnp.sum(e, axis=0, keepdims=True)
                total = part if total is None else total + part
            live = jnp.where(first_half, jnp.where(own_live[2 * a], 1.0, 0.0).astype(F32),
                             jnp.where(own_live[2 * a + 1], 1.0, 0.0).astype(F32)) > 0.5
            log_sum = jnp.where(live, top * exp_scale + jnp.log(total) * math.log2(math.e), -NEG)
            delta = delta_all[:, rows]
            stat_own[a:a + 1, :] = jnp.where(live, 1.0 / total, 0.0)
            stat_own[2 + a:3 + a, :] = delta
            for r, stat in enumerate((log_sum, delta)):
                for i in range(2):
                    at = 4 * a + 2 * r + i
                    stat_out[h, at:at + 1, :] = stat[:, block(i)]
                    if a == 0:
                        stat_even[h, at:at + 1, :] = stat[:, block(i)]

    def grad_part(h):
        keys, vals = own[h, KEY], own[h, VAL]
        far_keys = kv_in[h, :, 0].reshape(w * BLK, HD)
        far_vals = kv_in[h, :, 1].reshape(w * BLK, HD)
        for a in range(2):
            near, rows = half(a)
            grad = own[h, GRD, rows]
            dp_buf[0:near * BLK] = dot(vals[:near * BLK], grad, both_last)
            dp_buf[4 * BLK:] = dot(far_vals, grad, both_last)
            scale, delta = stat_own[a:a + 1, :], stat_own[2 + a:3 + a, :]
            for b in list(range(near)) + [4 + t for t in range(w)]:
                prob = s_buf[block(b), rows] * scale
                if b < 4:
                    p_buf[block(b), rows] = prob.astype(BF16)
                ds_buf[block(b), rows] = (prob * (dp_buf[block(b)] - delta)).astype(BF16)
            dq = dot(ds_buf[0:near * BLK, rows], keys[:near * BLK], ((0,), (0,)))
            dq += dot(ds_buf[4 * BLK:, rows], far_keys, ((0,), (0,)))
            stage[h, 0, rows] = (dq * inv_root).astype(BF16)

    def own_keys(h):
        second = slice(SL, 2 * SL)
        query, grad = own[h, QRY], own[h, GRD]
        part_own[h, 0, 0:SL] = dot(ds_buf[0:SL], query, nat)
        part_own[h, 0, second] = dot(ds_buf[second, second], query[second], nat)
        part_own[h, 1, 0:SL] = dot(p_buf[0:SL], grad, nat)
        part_own[h, 1, second] = dot(p_buf[second, second], grad[second], nat)

    def key_side(h):
        queries = qg_in[h, :, 0].reshape(w * BLK, HD)
        grads = qg_in[h, :, 1].reshape(w * BLK, HD)
        dk, dv = part_own[h, 0], part_own[h, 1]
        for low in range(0, w, 2):
            at = slice(low * BLK, min(low + 2, w) * BLK)
            sk_buf[:, at] = dot(own[h, KEY], queries[at], both_last)
            dpk_buf[:, at] = dot(own[h, VAL], grads[at], both_last)
            for t in range(low, min(low + 2, w)):
                def stat(r):
                    def even_row(i):
                        return stat_near[h, 2 * r + i:2 * r + i + 1, :]

                    def odd_row(i):
                        return stat_near[h, 4 + 2 * r + i:5 + 2 * r + i, :]

                    row = numbered(t, row_from_even, even_row, odd_row)
                    if t >= w - 2:
                        i = w - 1 - t
                        row = jnp.where(row_passed[t], stat_far[h, 2 * r + i:2 * r + i + 1, :], row)
                    return row

                log_sum, delta = stat(0), stat(1)
                for b in range(4):
                    ok = row_own[t]
                    if b >= 2:
                        ok = jnp.logical_or(ok, row_passed[t])
                    level = jnp.where(jnp.logical_and(ok, own_live[b]), log_sum, -NEG)
                    prob = jnp.exp2(sk_buf[block(b), block(t)] * exp_scale - level)
                    pk_buf[block(b), block(t)] = prob.astype(BF16)
                    dsk_buf[block(b), block(t)] = (prob * (dpk_buf[block(b), block(t)] - delta)).astype(BF16)
            dv += dot(pk_buf[:, at], grads[at], nat)
            dk += dot(dsk_buf[:, at], queries[at], nat)
        stage[h, 2] = dv.astype(BF16)
        give(h, 2)
        stage[h, 1] = (dk * inv_root).astype(BF16)
        give(h, 1)

    @pl.when(jnp.logical_not(has_behind))
    def _():
        kv_in[...] = jnp.zeros_like(kv_in)

    @pl.when(jnp.logical_not(has_ahead))
    def _():
        qg_in[...] = jnp.zeros_like(qg_in)
        stat_near[...] = jnp.zeros_like(stat_near)

    @pl.when(jnp.logical_not(has_ahead_two))
    def _():
        stat_far[...] = jnp.zeros_like(stat_far)

    pl.semaphore_wait(barrier, met)
    for h in range(early):
        for a in (KEY, VAL, QRY, GRD):
            mate_in(h, a).start()

    def start_keys(h):
        fetched(h, (KEY, VAL))

        @when_ahead
        def _():
            make_a(h, (KEY, VAL), kv_out)
            keys_a(h).start()

    def start_rows(h):
        fetched(h, (QRY, GRD))

        @when_behind
        def _():
            make_a(h, (QRY, GRD), qg_out)
            rows_a(h).start()

    for h in range(early):
        start_keys(h)
        start_rows(h)

    for h in range(early):
        fetch(h, (OUT,))

    for h in range(early, min(early + 2, nh)):
        fetch(h, (KEY, VAL, QRY, GRD, OUT))

    def drain(h):
        for a in range(5):
            mate_in(h, a).wait_send()

        @when_ahead
        def _():
            keys_a(h).wait_send()
            for i in range(2):
                keys_b(h, i).wait_send()

        @when_behind
        def _():
            rows_a(h).wait_send()
            rows_b(h).wait_send()
            stats_near(h).wait_send()

        @when_behind_two
        def _():
            stats_far(h).wait_send()

        for a in range(3):
            local_res(h, a).wait()
            mate_res(h, a).wait_send()
            mate_res_arrival(h, a).wait_recv()

    @pl.loop(0, nh + DRAIN_LAG)
    def _(step):
        @pl.when(step < nh)
        def _():
            h = step

            @when_behind
            def _():
                keys_a(h).wait_recv()

            @when_ahead
            def _():
                make_b(h, (KEY, VAL), kv_in, kv_out, key_pass)
                for i in range(2):
                    keys_b(h, i).start()

        @pl.when(step + early < nh)
        def _():
            start_keys(step + early)

        @pl.when(step + early + 2 < nh)
        def _():
            fetch(step + early + 2, (KEY, VAL, QRY, GRD, OUT))

        @pl.when(jnp.logical_and(step >= QUERY_LAG, step < nh + QUERY_LAG))
        def _():
            h = step - QUERY_LAG
            fetched(h, (OUT,))

            @when_behind
            def _():
                keys_b(h, 0).wait_recv()

            soft_part(h)

            @when_behind
            def _():
                stats_near(h).start()

            @when_behind_two
            def _():
                stats_far(h).start()

        @pl.when(jnp.logical_and(step >= KEY_LAG, step < nh + KEY_LAG))
        def _():
            h = step - KEY_LAG

            @when_ahead
            def _():
                rows_b(h).wait_recv()
                stats_near(h).wait_recv()

            @when_ahead_two
            def _():
                stats_far(h).wait_recv()

            key_side(h)

        @pl.when(step < nh)
        def _():
            h = step

            @when_ahead
            def _():
                rows_a(h).wait_recv()

            @when_behind
            def _():
                make_b(h, (QRY, GRD), qg_in, qg_out, row_pass)
                rows_b(h).start()

        @pl.when(step + early < nh)
        def _():
            start_rows(step + early)

        @pl.when(jnp.logical_and(step >= QUERY_LAG, step < nh + QUERY_LAG))
        def _():
            h = step - QUERY_LAG

            @when_behind
            def _():
                keys_b(h, 1).wait_recv()

            grad_part(h)
            give(h, 0)
            own_keys(h)

        @pl.when(step >= DRAIN_LAG)
        def _():
            drain(step - DRAIN_LAG)


def fused(w, owners, queries, key_states, value_states, attn_out, out_grad):
    width = queries.shape[1]
    nh = width // (2 * HD)
    anywhere = pl.BlockSpec(memory_space=pl.ANY)
    dma = pltpu.SemaphoreType.DMA
    slots = pltpu.VMEM((nh, w, 2, BLK, HD), BF16)
    short = pltpu.VMEM((nh, 4, HD), F32)
    stats = pltpu.VMEM((nh, 8, HD), F32)
    return pl.pallas_call(
        functools.partial(kernel, w, nh),
        out_shape=[jax.ShapeDtypeStruct(queries.shape, BF16)] * 3,
        in_specs=[anywhere] * 6,
        out_specs=[anywhere] * 3,
        scratch_shapes=[
            pltpu.VMEM((nh, 5, 2 * SL, HD), BF16),
            slots, slots, slots, slots,
            stats, stats, short, short, pltpu.VMEM((8, SL), F32),
            pltpu.VMEM((nh, 2, 2 * SL, HD), F32),
            pltpu.VMEM((nh, 3, 2 * SL, HD), BF16),
            pltpu.VMEM(((4 + w) * BLK, 2 * SL), F32),
            pltpu.VMEM(((4 + w) * BLK, SL), F32),
            pltpu.VMEM((2 * SL, 2 * SL), BF16),
            pltpu.VMEM(((4 + w) * BLK, 2 * SL), BF16),
            pltpu.VMEM((2 * SL, w * BLK), F32),
            pltpu.VMEM((2 * SL, w * BLK), F32),
            pltpu.VMEM((2 * SL, w * BLK), BF16),
            pltpu.VMEM((2 * SL, w * BLK), BF16),
            pltpu.SMEM(owners.shape, jnp.int32), dma,
            dma((nh, 5)), dma((nh, 5)), dma((nh, 5)),
            dma((nh,)), dma((nh,)), dma((nh, 2)), dma((nh, 2)),
        ] + [dma((nh,))] * 8 + [dma((nh, 3))] * 3,
        compiler_params=pltpu.CompilerParams(
            collective_id=w - 4, has_side_effects=True, vmem_limit_bytes=56 * 2**20),
        name="slots%d" % w,
    )(owners, queries, key_states, value_states, attn_out, out_grad)


def place(a, b, c, x, y, z, sems):
    copies = [pltpu.make_async_copy(s, d, sems.at[i]) for i, (s, d) in enumerate(((a, x), (b, y), (c, z)))]
    for copy in copies:
        copy.start()
    for copy in copies:
        copy.wait()


def placed(arrays):
    anywhere = pl.BlockSpec(memory_space=pl.ANY)
    return pl.pallas_call(
        place, out_shape=[jax.ShapeDtypeStruct(a.shape, a.dtype) for a in arrays],
        in_specs=[anywhere] * 3, out_specs=[anywhere] * 3,
        scratch_shapes=[pltpu.SemaphoreType.DMA((3,))], name="place")(*arrays)


def per_device(queries, key_states, value_states, attn_out, out_grad, owner_ids):
    n_grp, n_seq = lax.axis_size("grp"), lax.axis_size("seq")
    shard = (owner_ids + n_seq * jnp.arange(n_grp, dtype=jnp.int32)[:, None]).reshape(-1, 1, 1)
    chip = jnp.arange(n_grp * n_seq // 2, dtype=jnp.int32)[None, :]
    around = 2 * chip + jnp.arange(-3, 5, dtype=jnp.int32)[:, None]
    m3, m2, m1, e0, o0, p2, p3, p4 = jnp.sum((shard == around).astype(jnp.int32), axis=0)
    most = jnp.max(jnp.maximum(sum(needs(m1, e0, o0, p2, p3, p4)), sum(needs(p2, o0, e0, m1, m2, m3))))
    return placed(lax.switch(
        most - 4,
        [functools.partial(fused, w) for w in (4, 5, 6)],
        owner_ids, queries, key_states, value_states, attn_out, out_grad))


def solution(mesh):
    rows = P(("grp", "seq"), None)
    return jax.shard_map(
        per_device,
        mesh=mesh,
        in_specs=(rows,) * 5 + (P(),),
        out_specs=(rows,) * 3,
        check_vma=False,
    )
```

```python
import functools
import math

import jax
import jax.numpy as jnp
from jax import lax
from jax.experimental import pallas as pl
from jax.experimental.pallas import tpu as pltpu
from jax.sharding import PartitionSpec as P

HD = 128
BLK = 128
SL = 256
MESH = pl.DeviceIdType.MESH
F32 = jnp.float32
BF16 = jnp.bfloat16
NEG = -1e30
LEAD, QUERY_LAG, KEY_LAG, DRAIN_LAG = 2, 1, 3, 5
KEY, VAL, QRY, GRD, OUT = range(5)


def dot(a, b, dims):
    return lax.dot_general(a, b, (dims, ((), ())), preferred_element_type=F32)


def needs(far, first, second, next_one, next_two, next_three):
    near_two = next_one + next_two
    return (jnp.where(next_one > 0, far, 0), jnp.where(near_two > 0, first, 0),
            jnp.where(near_two + next_three > 0, second, 0))


def kernel(w, nh, owners_in, q_in, k_in, v_in, o_in, g_in, dq_out, dk_out, dv_out,
           own, kv_out, kv_in, qg_out, qg_in, stat_out, stat_near, stat_even, stat_far, stat_own, part_own, stage,
           s_buf, dp_buf, p_buf, ds_buf, sk_buf, dpk_buf, pk_buf, dsk_buf,
           owners, owners_sem, loc_sem, xs_sem, xr_sem, kas_sem, kar_sem, kbs_sem, kbr_sem, qas_sem, qar_sem, qbs_sem, qbr_sem,
           sns_sem, snr_sem, sfs_sem, sfr_sem, ol_sem, os_sem, or_sem):
    n_seq = lax.axis_size("seq")
    n_all = lax.axis_size("grp") * n_seq
    me = lax.axis_index("grp") * n_seq + lax.axis_index("seq")
    core = lax.rem(me, 2)
    even = me - core
    na = w - 2

    def dev(d):
        d = lax.rem(d + n_all, n_all)
        return (d // n_seq, lax.rem(d, n_seq))

    def only(cond):
        return lambda act: pl.when(cond)(act)

    mate = dev(even + 1 - core)
    ahead, ahead_two, behind, behind_two = [dev(me + i) for i in (2, 4, -2, -4)]
    has_ahead, has_ahead_two = me < n_all - 2, me < n_all - 4
    has_behind, has_behind_two = me >= 2, me >= 4
    when_ahead, when_ahead_two = only(has_ahead), only(has_ahead_two)
    when_behind, when_behind_two = only(has_behind), only(has_behind_two)

    barrier = pltpu.get_barrier_semaphore()
    pl.semaphore_signal(barrier, inc=1, device_id=mate, device_id_type=MESH)
    met = jnp.int32(1)
    for there, other in ((has_ahead, ahead), (has_behind, behind), (has_ahead_two, ahead_two), (has_behind_two, behind_two)):
        @pl.when(there)
        def _():
            pl.semaphore_signal(barrier, inc=1, device_id=other, device_id_type=MESH)

        met += there.astype(jnp.int32)

    owners_copy = pltpu.make_async_copy(owners_in, owners, owners_sem)
    owners_copy.start()

    inputs = (k_in, v_in, q_in, g_in, o_in)
    outputs = (dq_out, dk_out, dv_out)

    def cols(which_core, h):
        return pl.ds(pl.multiple_of((which_core * nh + h) * HD, HD), HD)

    mine = pl.ds(pl.multiple_of(core * SL, SL), SL)
    mates = pl.ds(pl.multiple_of((1 - core) * SL, SL), SL)

    def local_in(h, a):
        return pltpu.make_async_copy(inputs[a].at[:, cols(core, h)], own.at[h, a, mine], loc_sem.at[h, a])

    def mate_in(h, a):
        return pltpu.make_async_remote_copy(
            src_ref=inputs[a].at[:, cols(1 - core, h)], dst_ref=own.at[h, a, mine],
            send_sem=xs_sem.at[h, a], recv_sem=xr_sem.at[h, a], device_id=mate, device_id_type=MESH)

    def mate_in_arrival(h, a):
        return pltpu.make_async_remote_copy(
            src_ref=own.at[h, a, mates], dst_ref=own.at[h, a, mates],
            send_sem=xs_sem.at[h, a], recv_sem=xr_sem.at[h, a], device_id=mate, device_id_type=MESH)

    def hop(src, dst, h, lo, size, ss, rs, to):
        return pltpu.make_async_remote_copy(
            src_ref=src.at[h, pl.ds(lo, size)], dst_ref=dst.at[h, pl.ds(lo, size)],
            send_sem=ss.at[h], recv_sem=rs.at[h], device_id=to, device_id_type=MESH)

    def keys_a(h):
        return hop(kv_out, kv_in, h, 0, na, kas_sem, kar_sem, ahead)

    def keys_b(h, i):
        return pltpu.make_async_remote_copy(
            src_ref=kv_out.at[h, pl.ds(na, 2), i], dst_ref=kv_in.at[h, pl.ds(na, 2), i],
            send_sem=kbs_sem.at[h, i], recv_sem=kbr_sem.at[h, i], device_id=ahead, device_id_type=MESH)

    def rows_a(h):
        return hop(qg_out, qg_in, h, 0, na, qas_sem, qar_sem, behind)

    def rows_b(h):
        return hop(qg_out, qg_in, h, na, 2, qbs_sem, qbr_sem, behind)

    def stats_near(h):
        return hop(stat_out, stat_near, h, 0, 8, sns_sem, snr_sem, behind)

    def stats_far(h):
        return hop(stat_even, stat_far, h, 0, 4, sfs_sem, sfr_sem, behind_two)

    def local_res(h, a):
        return pltpu.make_async_copy(stage.at[h, a, mine], outputs[a].at[:, cols(core, h)], ol_sem.at[h, a])

    def mate_res(h, a):
        return pltpu.make_async_remote_copy(
            src_ref=stage.at[h, a, mates], dst_ref=outputs[a].at[:, cols(core, h)],
            send_sem=os_sem.at[h, a], recv_sem=or_sem.at[h, a], device_id=mate, device_id_type=MESH)

    def mate_res_arrival(h, a):
        return pltpu.make_async_remote_copy(
            src_ref=stage.at[h, a, mates], dst_ref=outputs[a].at[:, cols(1 - core, h)],
            send_sem=os_sem.at[h, a], recv_sem=or_sem.at[h, a], device_id=mate, device_id_type=MESH)

    def give(h, a):
        local_res(h, a).start()
        mate_res(h, a).start()

    def live_count(shard):
        s = jnp.clip(shard, 0, n_all - 1)
        total = jnp.int32(0)
        for b in range(owners.shape[1]):
            total += (owners[s // n_seq, b] == lax.rem(s, n_seq)).astype(jnp.int32)
        return jnp.where(jnp.logical_and(shard >= 0, shard < n_all), total, 0)

    early = min(LEAD, nh)
    for h in range(early):
        for a in (KEY, VAL, QRY, GRD):
            local_in(h, a).start()

    owners_copy.wait()
    m3, m2, m1, e0, o0, p2, p3, p4 = [live_count(even + i) for i in range(-3, 5)]
    own_live = (e0 >= 1, e0 >= 2, o0 >= 1, o0 >= 2)

    key_from_far, key_from_even, key_from_odd = needs(m3, m2, m1, e0, o0, p2)
    key_pass, key_even, key_odd = needs(m1, e0, o0, p2, p3, p4)
    row_from_far, row_from_odd, row_from_even = needs(p4, p3, p2, o0, e0, m1)
    row_pass, row_odd, row_even = needs(p2, o0, e0, m1, m2, m3)

    def arrivals(passed_count, own_count):
        passed, there = [], []
        for t in range(w):
            by_pass = jnp.bool_(False)
            if t == w - 1:
                by_pass = passed_count >= 1
            elif t == w - 2:
                by_pass = passed_count >= 2
            passed.append(by_pass)
            there.append(jnp.logical_and(jnp.logical_not(by_pass), own_count > t))
        return passed, there

    key_passed, key_own = arrivals(key_from_far, key_from_even + key_from_odd)
    row_passed, row_own = arrivals(row_from_far, row_from_even + row_from_odd)

    def fetch(h, a_list):
        for a in a_list:
            local_in(h, a).start()
            mate_in(h, a).start()

    def fetched(h, a_list):
        for a in a_list:
            local_in(h, a).wait()
            mate_in_arrival(h, a).wait_recv()

    def numbered(t, first_count, first, then):
        if t == 0:
            return jnp.where(first_count >= 1, first(0), then(0))
        if t == 1:
            return jnp.where(first_count >= 2, first(1), jnp.where(first_count >= 1, then(0), then(1)))
        if t == 2:
            return jnp.where(first_count >= 2, then(0), then(1))
        return then(1)

    def own_pick(h, x, t):
        def from_even(i):
            return own[h, x, i * BLK:(i + 1) * BLK, :]

        def from_odd(i):
            return own[h, x, (2 + i) * BLK:(3 + i) * BLK, :]

        if x in (KEY, VAL):
            return numbered(t, key_odd, from_odd, from_even)
        return numbered(t, row_even, from_even, from_odd)

    def make_a(h, pair, out):
        for t in range(na):
            for i, x in enumerate(pair):
                out[h, t, i] = own_pick(h, x, t)

    def make_b(h, pair, arrived, out, passed_count):
        for i, x in enumerate(pair):
            first, second = arrived[h, 0, i], arrived[h, 1, i]
            if w - 2 < 4:
                second = jnp.where(passed_count >= 2, second, own_pick(h, x, w - 2))
            if w - 1 < 4:
                first = jnp.where(passed_count >= 1, first, own_pick(h, x, w - 1))
            out[h, w - 2, i] = second
            out[h, w - 1, i] = first

    inv_root = HD ** (-0.5)
    exp_scale = inv_root * math.log2(math.e)
    row_id = lax.broadcasted_iota(jnp.int32, (BLK, SL), 0)
    col_id = lax.broadcasted_iota(jnp.int32, (BLK, SL), 1)
    first_half = lax.broadcasted_iota(jnp.int32, (1, SL), 1) < BLK
    nat, both_last = ((1,), (0,)), ((1,), (1,))

    def block(b):
        return slice(b * BLK, (b + 1) * BLK)

    def half(a):
        return 2 * (a + 1), slice(a * SL, (a + 1) * SL)

    def early_part(h):
        keys = own[h, KEY]
        first_keys = kv_in[h, 0:na, 0].reshape(na * BLK, HD)
        prod = own[h, GRD].astype(F32) * own[h, OUT].astype(F32)
        delta_all = jnp.sum(prod.T, axis=0, keepdims=True)
        for a in range(2):
            near, rows = half(a)
            query = own[h, QRY, rows]
            stat_own[2 + a:3 + a, :] = delta_all[:, rows]
            s_buf[0:near * BLK, rows] = dot(keys[:near * BLK], query, both_last)
            s_buf[4 * BLK:(4 + na) * BLK, rows] = dot(first_keys, query, both_last)

    def soft_part(h):
        late_keys = kv_in[h, na:w, 0].reshape(2 * BLK, HD)
        for a in range(2):
            rows = half(a)[1]
            s_buf[(4 + na) * BLK:, rows] = dot(late_keys, own[h, QRY, rows], both_last)
        for a in range(2):
            near, rows = half(a)
            blocks = list(range(near)) + [4 + t for t in range(w)]
            allowed = []
            for b in blocks:
                ok = own_live[b] if b < 4 else key_own[b - 4]
                if b >= 4 and a == 0:
                    ok = jnp.logical_or(ok, key_passed[b - 4])
                allowed.append(ok)
            top = None
            for b, ok in zip(blocks, allowed):
                x = s_buf[block(b), rows]
                if b < 4 and b >= 2 * a:
                    x = jnp.where(row_id + (b - 2 * a) * BLK <= col_id, x, NEG)
                    s_buf[block(b), rows] = x
                high = jnp.max(x, axis=0, keepdims=True) + jnp.where(ok, 0.0, NEG).astype(F32)
                top = high if top is None else jnp.maximum(top, high)
            total = None
            for b, ok in zip(blocks, allowed):
                e = jnp.exp2((s_buf[block(b), rows] - jnp.where(ok, top, -NEG)) * exp_scale)
                s_buf[block(b), rows] = e
                part = jnp.sum(e, axis=0, keepdims=True)
                total = part if total is None else total + part
            live = jnp.where(first_half, jnp.where(own_live[2 * a], 1.0, 0.0).astype(F32),
                             jnp.where(own_live[2 * a + 1], 1.0, 0.0).astype(F32)) > 0.5
            log_sum = jnp.where(live, top * exp_scale + jnp.log(total) * math.log2(math.e), -NEG)
            delta = stat_own[2 + a:3 + a, :]
            stat_own[a:a + 1, :] = jnp.where(live, 1.0 / total, 0.0)
            for r, stat in enumerate((log_sum, delta)):
                for i in range(2):
                    at = 4 * a + 2 * r + i
                    stat_out[h, at:at + 1, :] = stat[:, block(i)]
                    if a == 0:
                        stat_even[h, at:at + 1, :] = stat[:, block(i)]

    def grad_part(h):
        keys, vals = own[h, KEY], own[h, VAL]
        far_keys = kv_in[h, :, 0].reshape(w * BLK, HD)
        far_vals = kv_in[h, :, 1].reshape(w * BLK, HD)
        for a in range(2):
            near, rows = half(a)
            grad = own[h, GRD, rows]
            dp_buf[0:near * BLK] = dot(vals[:near * BLK], grad, both_last)
            dp_buf[4 * BLK:] = dot(far_vals, grad, both_last)
            scale, delta = stat_own[a:a + 1, :], stat_own[2 + a:3 + a, :]
            for b in list(range(near)) + [4 + t for t in range(w)]:
                prob = s_buf[block(b), rows] * scale
                if b < 4:
                    p_buf[block(b), rows] = prob.astype(BF16)
                ds_buf[block(b), rows] = (prob * (dp_buf[block(b)] - delta)).astype(BF16)
            dq = dot(ds_buf[0:near * BLK, rows], keys[:near * BLK], ((0,), (0,)))
            dq += dot(ds_buf[4 * BLK:, rows], far_keys, ((0,), (0,)))
            stage[h, 0, rows] = (dq * inv_root).astype(BF16)

    def own_keys(h):
        second = slice(SL, 2 * SL)
        query, grad = own[h, QRY], own[h, GRD]
        part_own[h, 0, 0:SL] = dot(ds_buf[0:SL], query, nat)
        part_own[h, 0, second] = dot(ds_buf[second, second], query[second], nat)
        part_own[h, 1, 0:SL] = dot(p_buf[0:SL], grad, nat)
        part_own[h, 1, second] = dot(p_buf[second, second], grad[second], nat)

    def key_side(h):
        queries = qg_in[h, :, 0].reshape(w * BLK, HD)
        grads = qg_in[h, :, 1].reshape(w * BLK, HD)
        dk, dv = part_own[h, 0], part_own[h, 1]
        for low in range(0, w, 2):
            at = slice(low * BLK, min(low + 2, w) * BLK)
            sk_buf[:, at] = dot(own[h, KEY], queries[at], both_last)
            dpk_buf[:, at] = dot(own[h, VAL], grads[at], both_last)
            for t in range(low, min(low + 2, w)):
                def stat(r):
                    def even_row(i):
                        return stat_near[h, 2 * r + i:2 * r + i + 1, :]

                    def odd_row(i):
                        return stat_near[h, 4 + 2 * r + i:5 + 2 * r + i, :]

                    row = numbered(t, row_from_even, even_row, odd_row)
                    if t >= w - 2:
                        i = w - 1 - t
                        row = jnp.where(row_passed[t], stat_far[h, 2 * r + i:2 * r + i + 1, :], row)
                    return row

                log_sum, delta = stat(0), stat(1)
                for b in range(4):
                    ok = row_own[t]
                    if b >= 2:
                        ok = jnp.logical_or(ok, row_passed[t])
                    level = jnp.where(jnp.logical_and(ok, own_live[b]), log_sum, -NEG)
                    prob = jnp.exp2(sk_buf[block(b), block(t)] * exp_scale - level)
                    pk_buf[block(b), block(t)] = prob.astype(BF16)
                    dsk_buf[block(b), block(t)] = (prob * (dpk_buf[block(b), block(t)] - delta)).astype(BF16)
            dv += dot(pk_buf[:, at], grads[at], nat)
            dk += dot(dsk_buf[:, at], queries[at], nat)
        stage[h, 2] = dv.astype(BF16)
        give(h, 2)
        stage[h, 1] = (dk * inv_root).astype(BF16)
        give(h, 1)

    @pl.when(jnp.logical_not(has_behind))
    def _():
        kv_in[...] = jnp.zeros_like(kv_in)

    @pl.when(jnp.logical_not(has_ahead))
    def _():
        qg_in[...] = jnp.zeros_like(qg_in)
        stat_near[...] = jnp.zeros_like(stat_near)

    @pl.when(jnp.logical_not(has_ahead_two))
    def _():
        stat_far[...] = jnp.zeros_like(stat_far)

    pl.semaphore_wait(barrier, met)
    for h in range(early):
        for a in (KEY, VAL, QRY, GRD):
            mate_in(h, a).start()

    def start_keys(h):
        fetched(h, (KEY, VAL))

        @when_ahead
        def _():
            make_a(h, (KEY, VAL), kv_out)
            keys_a(h).start()

    def start_rows(h):
        fetched(h, (QRY, GRD))

        @when_behind
        def _():
            make_a(h, (QRY, GRD), qg_out)
            rows_a(h).start()

    for h in range(early):
        start_keys(h)
        start_rows(h)

    for h in range(early):
        fetch(h, (OUT,))

    for h in range(early, min(early + 2, nh)):
        fetch(h, (KEY, VAL, QRY, GRD, OUT))

    def drain(h):
        for a in range(5):
            mate_in(h, a).wait_send()

        @when_ahead
        def _():
            keys_a(h).wait_send()
            for i in range(2):
                keys_b(h, i).wait_send()

        @when_behind
        def _():
            rows_a(h).wait_send()
            rows_b(h).wait_send()
            stats_near(h).wait_send()

        @when_behind_two
        def _():
            stats_far(h).wait_send()

        for a in range(3):
            local_res(h, a).wait()
            mate_res(h, a).wait_send()
            mate_res_arrival(h, a).wait_recv()

    @pl.loop(0, nh + DRAIN_LAG)
    def _(step):
        @pl.when(step < nh)
        def _():
            h = step

            @when_behind
            def _():
                keys_a(h).wait_recv()

            @when_ahead
            def _():
                make_b(h, (KEY, VAL), kv_in, kv_out, key_pass)
                for i in range(2):
                    keys_b(h, i).start()

        @pl.when(step + early < nh)
        def _():
            start_keys(step + early)

        @pl.when(step + early + 2 < nh)
        def _():
            fetch(step + early + 2, (KEY, VAL, QRY, GRD, OUT))

        @pl.when(jnp.logical_and(step >= QUERY_LAG, step < nh + QUERY_LAG))
        def _():
            h = step - QUERY_LAG
            fetched(h, (OUT,))
            early_part(h)

            @when_behind
            def _():
                keys_b(h, 0).wait_recv()

            soft_part(h)

            @when_behind_two
            def _():
                stats_far(h).start()

            @when_behind
            def _():
                stats_near(h).start()

        @pl.when(jnp.logical_and(step >= KEY_LAG, step < nh + KEY_LAG))
        def _():
            h = step - KEY_LAG

            @when_ahead
            def _():
                rows_b(h).wait_recv()
                stats_near(h).wait_recv()

            @when_ahead_two
            def _():
                stats_far(h).wait_recv()

            key_side(h)

        @pl.when(step < nh)
        def _():
            h = step

            @when_ahead
            def _():
                rows_a(h).wait_recv()

            @when_behind
            def _():
                make_b(h, (QRY, GRD), qg_in, qg_out, row_pass)
                rows_b(h).start()

        @pl.when(step + early < nh)
        def _():
            start_rows(step + early)

        @pl.when(jnp.logical_and(step >= QUERY_LAG, step < nh + QUERY_LAG))
        def _():
            h = step - QUERY_LAG

            @when_behind
            def _():
                keys_b(h, 1).wait_recv()

            grad_part(h)
            give(h, 0)
            own_keys(h)

        @pl.when(step >= DRAIN_LAG)
        def _():
            drain(step - DRAIN_LAG)


def fused(w, owners, queries, key_states, value_states, attn_out, out_grad):
    width = queries.shape[1]
    nh = width // (2 * HD)
    anywhere = pl.BlockSpec(memory_space=pl.ANY)
    dma = pltpu.SemaphoreType.DMA
    slots = pltpu.VMEM((nh, w, 2, BLK, HD), BF16)
    short = pltpu.VMEM((nh, 4, HD), F32)
    stats = pltpu.VMEM((nh, 8, HD), F32)
    return pl.pallas_call(
        functools.partial(kernel, w, nh),
        out_shape=[jax.ShapeDtypeStruct(queries.shape, BF16)] * 3,
        in_specs=[anywhere] * 6,
        out_specs=[anywhere] * 3,
        scratch_shapes=[
            pltpu.VMEM((nh, 5, 2 * SL, HD), BF16),
            slots, slots, slots, slots,
            stats, stats, short, short, pltpu.VMEM((8, SL), F32),
            pltpu.VMEM((nh, 2, 2 * SL, HD), F32),
            pltpu.VMEM((nh, 3, 2 * SL, HD), BF16),
            pltpu.VMEM(((4 + w) * BLK, 2 * SL), F32),
            pltpu.VMEM(((4 + w) * BLK, SL), F32),
            pltpu.VMEM((2 * SL, 2 * SL), BF16),
            pltpu.VMEM(((4 + w) * BLK, 2 * SL), BF16),
            pltpu.VMEM((2 * SL, w * BLK), F32),
            pltpu.VMEM((2 * SL, w * BLK), F32),
            pltpu.VMEM((2 * SL, w * BLK), BF16),
            pltpu.VMEM((2 * SL, w * BLK), BF16),
            pltpu.SMEM(owners.shape, jnp.int32), dma,
            dma((nh, 5)), dma((nh, 5)), dma((nh, 5)),
            dma((nh,)), dma((nh,)), dma((nh, 2)), dma((nh, 2)),
        ] + [dma((nh,))] * 8 + [dma((nh, 3))] * 3,
        compiler_params=pltpu.CompilerParams(
            collective_id=w - 4, has_side_effects=True, vmem_limit_bytes=56 * 2**20),
        name="slots%d" % w,
    )(owners, queries, key_states, value_states, attn_out, out_grad)


def place(a, b, c, x, y, z, sems):
    copies = [pltpu.make_async_copy(s, d, sems.at[i]) for i, (s, d) in enumerate(((a, x), (b, y), (c, z)))]
    for copy in copies:
        copy.start()
    for copy in copies:
        copy.wait()


def placed(arrays):
    anywhere = pl.BlockSpec(memory_space=pl.ANY)
    return pl.pallas_call(
        place, out_shape=[jax.ShapeDtypeStruct(a.shape, a.dtype) for a in arrays],
        in_specs=[anywhere] * 3, out_specs=[anywhere] * 3,
        scratch_shapes=[pltpu.SemaphoreType.DMA((3,))], name="place")(*arrays)


def per_device(queries, key_states, value_states, attn_out, out_grad, owner_ids):
    n_grp, n_seq = lax.axis_size("grp"), lax.axis_size("seq")
    shard = (owner_ids + n_seq * jnp.arange(n_grp, dtype=jnp.int32)[:, None]).reshape(-1, 1, 1)
    chip = jnp.arange(n_grp * n_seq // 2, dtype=jnp.int32)[None, :]
    around = 2 * chip + jnp.arange(-3, 5, dtype=jnp.int32)[:, None]
    m3, m2, m1, e0, o0, p2, p3, p4 = jnp.sum((shard == around).astype(jnp.int32), axis=0)
    most = jnp.max(jnp.maximum(sum(needs(m1, e0, o0, p2, p3, p4)), sum(needs(p2, o0, e0, m1, m2, m3))))
    return placed(lax.switch(
        most - 4,
        [functools.partial(fused, w) for w in (4, 5, 6)],
        owner_ids, queries, key_states, value_states, attn_out, out_grad))


def solution(mesh):
    rows = P(("grp", "seq"), None)
    return jax.shard_map(
        per_device,
        mesh=mesh,
        in_specs=(rows,) * 5 + (P(),),
        out_specs=(rows,) * 3,
        check_vma=False,
    )
```
